512 devices in a mesh: slot: 16 (over y_hi, x, core), blk: 32 (over z, y_lo).
Axes of the slice: x: 4, y: 4 (y_hi: 2, y_lo: 2; y = y_hi * 2 + y_lo), z: 16, core: 2. Of those that a mesh axis runs over, the one named last changes fastest.
Arguments:
- owner: int32 [16], replicated, may hold values from 0 to 15, as said below
- factor: float32 [16, 3584, 3584], P('slot', 'blk'), may hold values from -0.09375 to 0.09375
- inverse_old: bfloat16 [16, 3584, 3584], P('slot', 'blk'), may hold values from -1 to 1
- acts_t: bfloat16 [16, 3584, 640], P('slot', 'blk'), may hold values from -6 to 6
- damping: float32 [16], P('slot'), may hold values from 0.5 to 2
Outputs:
- refreshed: bfloat16 [16, 3584, 640], P('slot', 'blk')
The draws below stay inside these ranges and needn't reach their ends.
Inputs may be any that keep to these rules, and one draw needn't show every extreme that they name: owner names every index of slot exactly once, and for at least one layer l, owner[l] = (l + 8) mod 16.
All inputs are finite; a program needn't handle non-finite values.
Results may differ from the reference program's by a relative error of at most 0.0049.
Values may be sent and summed in bfloat16 or wider, within the bound.
A program may use at most 64 MiB of HBM per device.

```python
import math
import jax
import jax.numpy as jnp
from jax import lax

D = 3584
TOK = 640
COLS = 640
LAYERS = 16


def draw_owner(key, part):
    key = jax.random.fold_in(key, 7)
    perm_key, pick_key = jax.random.split(key)
    ordering = jax.random.permutation(perm_key, LAYERS).astype(jnp.int32)
    position = jax.random.randint(pick_key, (), 0, LAYERS).astype(jnp.int32)
    wanted = (position + LAYERS // 2) % LAYERS
    places = jnp.arange(LAYERS, dtype=jnp.int32)
    holder = jnp.sum(jnp.where(ordering == wanted, places, 0)).astype(jnp.int32)
    current = jnp.sum(jnp.where(places == position, ordering, 0)).astype(jnp.int32)
    swapped = jnp.where(places == holder, current, ordering)
    swapped = jnp.where(places == position, wanted, swapped)
    return swapped.astype(jnp.int32)


def block_scale(rng, extent, cuts, smallest, high):
    level, own = 1.0, jax.random.fold_in(rng, 6)
    for axis_at, shards_of in cuts:
        draws = jnp.exp(jax.random.uniform(jax.random.fold_in(own, axis_at), (shards_of,), jnp.float32, smallest / len(cuts), high / len(cuts)))
        level = level * jnp.repeat(draws, extent[axis_at] // shards_of).reshape([-1 if axis == axis_at else 1 for axis in range(len(extent))])
    return level


def gaussian(own_key, extent, deviation, most, shards=(), held_as=jnp.bfloat16):
    loudness = block_scale(own_key, extent, shards, -0.22, 0.18) if shards else 1.0
    result = jax.random.normal(own_key, extent, jnp.float32) * deviation * loudness
    return jnp.minimum(jnp.maximum(result, -most), most).astype(held_as)


def setup_inputs(seed: int = 0) -> dict:
    arg_keys = jax.random.split(jax.random.key(seed), 6)
    return {
        "owner": draw_owner(jax.random.fold_in(arg_keys[5], 71), 0),
        "factor": gaussian(arg_keys[1], (LAYERS, D, D), D ** -0.5, 0.09375, ((0, 16), (1, 32)), jnp.float32),
        "inverse_old": gaussian(arg_keys[2], (LAYERS, D, D), 0.125, 1.0, ((0, 16), (1, 32))),
        "acts_t": gaussian(arg_keys[3], (LAYERS, D, TOK), 1.0, 6.0, ((0, 16), (1, 32))),
        "damping": jnp.clip(jnp.exp(math.log(2.0) - 1.3862944 * jax.random.uniform(arg_keys[4], (LAYERS,), jnp.float32) ** block_scale(arg_keys[4], (LAYERS,), ((0, 16),), -0.2, 0.2)), 0.5, 2.0),
    }


beta_keep = 0.75


def refresh(layer_arrays):
    factor_panel, inverse_panel, acts_panel, damp_value = layer_arrays
    outer_full = jnp.dot(acts_panel, acts_panel.T, preferred_element_type=jnp.float32)
    damped = beta_keep * factor_panel + ((1.0 - beta_keep) / TOK) * outer_full + damp_value * jnp.eye(D, dtype=jnp.float32)
    window = inverse_panel[:, :COLS]
    applied = jnp.dot(damped, window.astype(jnp.float32), precision=lax.Precision.HIGHEST).astype(jnp.bfloat16)
    product = jnp.dot(inverse_panel, applied, preferred_element_type=jnp.float32)
    return (2.0 * window.astype(jnp.float32) - product).astype(jnp.bfloat16)


def reference(owner, factor, inverse_old, acts_t, damping):
    refreshed_panel = lax.map(refresh, (factor, inverse_old, acts_t, damping))
    return jnp.take(refreshed_panel, owner.astype(jnp.int32), axis=0)
```

```python
import jax
import jax.numpy as jnp
from jax import lax
from jax.experimental import pallas as pl
from jax.experimental.pallas import tpu as pltpu
from jax.sharding import PartitionSpec as P

COLS = 640
TOK = 640
BETA = 0.75
NZ = 16
NS = 16
ROWS = 112
KP = 128
PIECES = 7
MESH = pl.DeviceIdType.MESH
HOPS = NZ // 2
PARTS = ((0, 256), (256, 384))


def wait_for(ref, sem):
    pltpu.make_async_copy(ref, ref, sem).wait()


def kernel(
    owner, damping, factor, inverse, acts, out,
    f_in, p_in, f_out, p_out, f_work, p_work, a_own,
    w_ring, a_ring, x_ring, total, sibling_part, damp_out, damp_in,
    gathered, picked, load_sem,
    swap_send, swap_recv, ring_send, ring_recv, pair_send, pair_recv,
    give_send, give_recv, pick_send, pick_recv,
):
    slot = lax.axis_index("slot")
    blk = lax.axis_index("blk")
    chip = slot // 2
    core = slot % 2
    z = blk // 2
    side = blk % 2
    same = core == side

    def at(core_at, side_at, z_at):
        return (chip * 2 + core_at, z_at * 2 + side_at)

    sibling = at(1 - core, side, z)
    up = at(core, side, (z + 1) % NZ)
    down = at(core, side, (z + NZ - 1) % NZ)

    f_load = pltpu.make_async_copy(factor.at[0], f_in, load_sem.at[0])
    p_load = pltpu.make_async_copy(inverse.at[0], p_in, load_sem.at[1])
    f_load.start()
    p_load.start()

    barrier = pltpu.get_barrier_semaphore()
    pl.semaphore_signal(barrier, inc=1, device_id=up, device_id_type=MESH)
    pl.semaphore_signal(barrier, inc=1, device_id=down, device_id_type=MESH)

    def greet(i, carry):
        @pl.when(jnp.logical_or(i // 2 != slot, i % 2 != side))
        def _():
            pl.semaphore_signal(
                barrier, inc=1, device_id=(i // 2, z * 2 + i % 2), device_id_type=MESH
            )
        return carry

    lax.fori_loop(0, 2 * NS, greet, 0)

    pad = jnp.zeros((KP - ROWS, COLS), jnp.bfloat16)

    def clear(i, carry):
        w_ring[i, ROWS:KP, :] = pad
        a_ring[i, ROWS:KP, :] = pad
        x_ring[i, ROWS:KP, :] = pad
        return carry

    lax.fori_loop(0, NZ, clear, 0)
    pl.semaphore_wait(barrier, 2 * NS + 1)

    def deliver(src, dst, send, recv, target, own):
        @pl.when(own)
        def _():
            pltpu.make_async_copy(src, dst, recv).start()

        @pl.when(jnp.logical_not(own))
        def _():
            pltpu.make_async_remote_copy(
                src_ref=src, dst_ref=dst, send_sem=send, recv_sem=recv,
                device_id=target, device_id_type=MESH,
            ).start()

    def sent(src, send, own):
        @pl.when(jnp.logical_not(own))
        def _():
            wait_for(src, send)

    w_home = inverse.at[0, :, pl.ds(0, COLS)]
    a_home = acts.at[0]
    deliver(
        w_home, w_ring.at[z, pl.ds(0, ROWS)], swap_send.at[0], swap_recv.at[0],
        at(side, core, z), same,
    )
    own_rows = pl.ds(pl.multiple_of(side * ROWS, 16), ROWS)
    for q in range(2):
        deliver(
            a_home, a_own.at[own_rows], swap_send.at[1 + q], swap_recv.at[1 + side],
            at(q, core, z), jnp.logical_and(same, core == q),
        )

    damp_out[...] = jnp.full((8, 128), damping[0], jnp.float32)

    @pl.when(same)
    def _():
        damp_in[...] = damp_out[...]
        pltpu.make_async_remote_copy(
            src_ref=damp_out, dst_ref=damp_in, send_sem=swap_send.at[7],
            recv_sem=swap_recv.at[7], device_id=sibling, device_id_type=MESH,
        ).start()

    def relayout(src, dst):
        for j in range(2 * NZ):
            start = ROWS * j
            base = start // 128 * 128
            off = start - base
            if off == 0:
                piece = src[:, base : base + 128].astype(jnp.bfloat16)
            elif off + ROWS <= 128:
                piece = pltpu.roll(
                    src[:, base : base + 128].astype(jnp.float32), 128 - off, 1
                ).astype(jnp.bfloat16)
            else:
                piece = pltpu.roll(
                    src[:, base : base + 256].astype(jnp.float32), 256 - off, 1
                )[:, :128].astype(jnp.bfloat16)
            dst[j % 2, j // 2] = piece

    def send_panel(src, dst, first):
        for q in range(2):
            deliver(
                src.at[q], dst.at[:, own_rows], swap_send.at[first + q],
                swap_recv.at[first + side],
                at(q, core, z), jnp.logical_and(same, core == q),
            )

    f_load.wait()
    relayout(f_in, f_out)
    send_panel(f_out, f_work, 3)

    def ring_copy(stream, ref, place, way, hop):
        return pltpu.make_async_remote_copy(
            src_ref=ref, dst_ref=ref, send_sem=ring_send.at[stream, way, hop],
            recv_sem=ring_recv.at[stream, place],
            device_id=up if way == 0 else down, device_id_type=MESH,
        )

    def ring_ref(stream, place):
        if stream == 0:
            return w_ring.at[place, pl.ds(0, ROWS)]
        if stream == 1:
            return a_ring.at[place, pl.ds(0, ROWS)]
        first, width = PARTS[stream - 2]
        return x_ring.at[place, pl.ds(0, ROWS), pl.ds(first, width)]

    def far(stream):
        return (HOPS, HOPS - 1) if stream % 2 == 0 else (HOPS - 1, HOPS)

    def step(stream, hop):
        for way in range(2):
            if hop <= far(stream)[way]:
                place = (z - hop + NZ) % NZ if way == 0 else (z + hop) % NZ
                ref = ring_ref(stream, place)
                if hop > 0:
                    wait_for(ref, ring_recv.at[stream, place])
                if hop < far(stream)[way]:
                    ring_copy(stream, ref, place, way, hop).start()

    def ring_sent(stream):
        for way in range(2):
            for hop in range(far(stream)[way]):
                place = (z - hop + NZ) % NZ if way == 0 else (z + hop) % NZ
                wait_for(ring_ref(stream, place), ring_send.at[stream, way, hop])

    def first_product(place):
        outer = lax.dot_general(
            a_own[...], a_ring[place], (((1,), (1,)), ((), ())),
            preferred_element_type=jnp.float32,
        )
        damped = BETA * f_work[place].astype(jnp.float32) + ((1.0 - BETA) / TOK) * outer
        total[...] += jnp.dot(
            damped.astype(jnp.bfloat16), w_ring[place], preferred_element_type=jnp.float32
        )

    def second_product(place):
        total[...] += jnp.dot(
            p_work[place], x_ring[place], preferred_element_type=jnp.float32
        )

    def both(product, hop):
        if hop == 0:
            product(z)
        elif hop == HOPS:
            product((z + HOPS) % NZ)
        else:
            def one(s, carry):
                product((z + NZ + (1 - 2 * s) * hop) % NZ)
                return carry
            lax.fori_loop(0, 2, one, 0)

    wait_for(w_ring.at[z, pl.ds(0, ROWS)], swap_recv.at[0])
    step(0, 0)
    for b in range(2):
        wait_for(a_own.at[pl.ds(b * ROWS, ROWS)], swap_recv.at[1 + b])
    mine = pl.ds(pl.multiple_of(core * ROWS, 16), ROWS)
    other = pl.ds(pl.multiple_of((1 - core) * ROWS, 16), ROWS)
    a_ring[z, 0:ROWS, :] = a_own[mine, :]
    step(1, 0)

    p_load.wait()
    relayout(p_in, p_out)
    send_panel(p_out, p_work, 5)

    total[...] = jnp.zeros_like(total)
    computed = 0
    for hop in range(1, HOPS + 1):
        step(0, hop)
        step(1, hop)
        if hop == 4:
            for b in range(2):
                wait_for(f_work.at[:, pl.ds(b * ROWS, ROWS)], swap_recv.at[3 + b])
        if hop >= 4:
            for _ in range(2):
                if computed <= hop:
                    both(first_product, computed)
                    computed += 1
    while computed <= HOPS:
        both(first_product, computed)
        computed += 1

    def pair_up(which):
        copy = pltpu.make_async_remote_copy(
            src_ref=total.at[other], dst_ref=sibling_part.at[which],
            send_sem=pair_send.at[which], recv_sem=pair_recv.at[which],
            device_id=sibling, device_id_type=MESH,
        )
        copy.start()
        copy.wait()

    @pl.when(jnp.logical_not(same))
    def _():
        wait_for(damp_in, swap_recv.at[7])

    pair_up(0)
    window = w_ring[z, 0:ROWS, :].astype(jnp.float32)
    applied = total[mine, :] + sibling_part[0] + damp_in[0:1, 0:1] * window
    x_ring[z, 0:ROWS, :] = applied.astype(jnp.bfloat16)
    step(2, 0)
    step(3, 0)
    total[...] = jnp.zeros_like(total)
    for b in range(2):
        wait_for(p_work.at[:, pl.ds(b * ROWS, ROWS)], swap_recv.at[5 + b])
    both(second_product, 0)
    for hop in range(1, HOPS + 1):
        step(2, hop)
        step(3, hop)
        both(second_product, hop)
    pair_up(1)
    fresh = 2.0 * window - (total[mine, :] + sibling_part[1])
    x_out = picked.at[0]
    x_out[0:ROWS, :] = fresh.astype(jnp.bfloat16)

    layer = chip * 2 + side
    for r in range(PIECES):
        target = 2 * r + r % 2
        deliver(
            x_out.at[pl.ds(r * 16, 16)], gathered.at[layer], give_send.at[r],
            give_recv.at[layer], (target, z * 2 + core),
            jnp.logical_and(slot == target, side == core),
        )

    piece = chip
    middle = jnp.logical_and(chip < PIECES, core == chip % 2)
    piece_rows = pl.ds(pl.multiple_of((chip % PIECES) * 16, 16), 16)

    @pl.when(middle)
    def _():
        for s in range(NS):
            wait_for(gathered.at[s], give_recv.at[s])
        for l in range(NS):
            picked[1, l * 16 : (l + 1) * 16, :] = gathered[owner[l]]
            deliver(
                picked.at[1, pl.ds(l * 16, 16)], out.at[0, piece_rows], pick_send.at[l],
                pick_recv.at[piece], (l, blk), slot == l,
            )

    for r in range(PIECES):
        wait_for(out.at[0, pl.ds(r * 16, 16)], pick_recv.at[r])

    sent(w_home, swap_send.at[0], same)
    for q in range(2):
        keep = jnp.logical_and(same, core == q)
        sent(a_home, swap_send.at[1 + q], keep)
        sent(f_out.at[q], swap_send.at[3 + q], keep)
        sent(p_out.at[q], swap_send.at[5 + q], keep)

    @pl.when(same)
    def _():
        wait_for(damp_out, swap_send.at[7])

    for stream in range(4):
        ring_sent(stream)
    for r in range(PIECES):
        sent(
            x_out.at[pl.ds(r * 16, 16)], give_send.at[r],
            jnp.logical_and(slot == 2 * r + r % 2, side == core),
        )

    @pl.when(middle)
    def _():
        for l in range(NS):
            sent(picked.at[1, pl.ds(l * 16, 16)], pick_send.at[l], slot == l)


def shards(owner, factor, inverse_old, acts_t, damping):
    bf16, f32 = jnp.bfloat16, jnp.float32
    dma = pltpu.SemaphoreType.DMA
    width = factor.shape[2]
    smem = pl.BlockSpec(memory_space=pltpu.SMEM)
    anywhere = pl.BlockSpec(memory_space=pl.ANY)
    return pl.pallas_call(
        kernel,
        out_shape=jax.ShapeDtypeStruct((1, ROWS, COLS), bf16),
        in_specs=[smem, smem, anywhere, anywhere, anywhere],
        out_specs=pl.BlockSpec(memory_space=pltpu.VMEM),
        scratch_shapes=[
            pltpu.VMEM((ROWS, width), f32),
            pltpu.VMEM((ROWS, width), bf16),
            pltpu.VMEM((2, NZ, ROWS, KP), bf16),
            pltpu.VMEM((2, NZ, ROWS, KP), bf16),
            pltpu.VMEM((NZ, 2 * ROWS, KP), bf16),
            pltpu.VMEM((NZ, 2 * ROWS, KP), bf16),
            pltpu.VMEM((2 * ROWS, TOK), bf16),
            pltpu.VMEM((NZ, KP, COLS), bf16),
            pltpu.VMEM((NZ, KP, TOK), bf16),
            pltpu.VMEM((NZ, KP, COLS), bf16),
            pltpu.VMEM((2 * ROWS, COLS), f32),
            pltpu.VMEM((2, ROWS, COLS), f32),
            pltpu.VMEM((8, 128), f32),
            pltpu.VMEM((8, 128), f32),
            pltpu.VMEM((NS, 16, COLS), bf16),
            pltpu.VMEM((2, 256, COLS), bf16),
            dma((2,)),
            dma((8,)),
            dma((8,)),
            dma((4, 2, HOPS)),
            dma((4, NZ)),
            dma((2,)),
            dma((2,)),
            dma((PIECES,)),
            dma((NS,)),
            dma((NS,)),
            dma((PIECES,)),
        ],
        compiler_params=pltpu.CompilerParams(
            collective_id=0, has_side_effects=True, vmem_limit_bytes=48 * 1024 * 1024
        ),
        cost_estimate=pl.CostEstimate(
            flops=2 * 3 * ROWS * width * COLS, bytes_accessed=3 * 1024 * 1024, transcendentals=0
        ),
    )(owner, damping, factor, inverse_old, acts_t)


def solution(mesh):
    placed = (
        P(),
        P("slot", "blk", None),
        P("slot", "blk", None),
        P("slot", "blk", None),
        P("slot"),
    )
    return jax.shard_map(
        shards, mesh=mesh, in_specs=placed, out_specs=P("slot", "blk", None), check_vma=False
    )
```

```python
import jax
import jax.numpy as jnp
from jax import lax
from jax.experimental import pallas as pl
from jax.experimental.pallas import tpu as pltpu
from jax.sharding import PartitionSpec as P

COLS = 640
TOK = 640
BETA = 0.75
NZ = 16
NS = 16
ROWS = 112
KP = 128
PIECES = 7
MESH = pl.DeviceIdType.MESH
HOPS = NZ // 2
PARTS = (384, 256)
FIRST = (0, 384)
STREAMS = ((128, 128, 128), (128, 128))
LONG_UP = (0, 3, 4, 6, 7)


def wait_for(ref, sem):
    pltpu.make_async_copy(ref, ref, sem).wait()


def kernel(
    owner_home, damping, factor, inverse, acts, out,
    owner, f_in, p_in, f_out, p_out, f_work, p_work, a_own, a_ring,
    w_ring, x_ring, total, sibling_part, fresh, gathered, picked,
    damp_out, damp_in, load_sem,
    swap_send, swap_recv, ring_send, ring_recv, pair_send, pair_recv,
    give_send, give_recv, pick_send, pick_recv, hello,
):
    slot = lax.axis_index("slot")
    blk = lax.axis_index("blk")
    chip = slot // 2
    core = slot % 2
    z = blk // 2
    side = blk % 2
    same = core == side

    def at(core_at, side_at, z_at):
        return (chip * 2 + core_at, z_at * 2 + side_at)

    sibling = at(1 - core, side, z)
    up = at(core, side, (z + 1) % NZ)
    down = at(core, side, (z + NZ - 1) % NZ)

    f_load = pltpu.make_async_copy(factor.at[0], f_in, load_sem.at[0])
    p_load = pltpu.make_async_copy(inverse.at[0], p_in, load_sem.at[1])
    f_load.start()
    p_load.start()
    owner_load = pltpu.make_async_copy(owner_home, owner, load_sem.at[2])
    owner_load.start()

    barrier = pltpu.get_barrier_semaphore()
    flips = [((chip + 4) % 8, core), (chip // 2 * 2 + 1 - chip % 2, core),
             (chip // 4 * 4 + (chip % 4 + 2) % 4, core)]
    partners = [up, down, sibling, at(core, 1 - side, z), at(1 - core, 1 - side, z)]
    far_partners = [(c * 2 + k, blk) for c, k in flips]
    for target in partners + far_partners:
        pl.semaphore_signal(barrier, inc=1, device_id=target, device_id_type=MESH)

    def greet(i):
        pl.semaphore_signal(
            hello.at[i], inc=1, device_id=far_partners[i], device_id_type=MESH
        )

    def greeted(i):
        pl.semaphore_wait(hello.at[i], 1)

    pad = jnp.zeros((KP - ROWS, COLS), jnp.bfloat16)

    def clear(i, carry):
        for p in range(2):
            a_ring[p][i, ROWS:KP, :] = pad[:, : PARTS[p]]
            w_ring[p][i, ROWS:KP, :] = pad[:, : PARTS[p]]
            for q, width in enumerate(STREAMS[p]):
                x_ring[p][q][i, ROWS:KP, :] = pad[:, :width]
        return carry

    lax.fori_loop(0, NZ, clear, 0)
    def relayout(src, dst):
        for j in range(2 * NZ):
            start = ROWS * j
            base = start // 128 * 128
            off = start - base
            if off == 0:
                piece = src[:, base : base + 128].astype(jnp.bfloat16)
            elif off + ROWS <= 128:
                piece = pltpu.roll(
                    src[:, base : base + 128].astype(jnp.float32), 128 - off, 1
                ).astype(jnp.bfloat16)
            else:
                piece = pltpu.roll(
                    src[:, base : base + 256].astype(jnp.float32), 256 - off, 1
                )[:, :128].astype(jnp.bfloat16)
            dst[j % 2, j // 2] = piece

    pl.semaphore_wait(barrier, len(partners) + len(far_partners))
    greet(0)

    pending = []

    def deliver(src, dst, send, recv, target, own):
        pending.append(lambda: sent(src, send, own))

        @pl.when(own)
        def _():
            pltpu.make_async_copy(src, dst, recv).start()

        @pl.when(jnp.logical_not(own))
        def _():
            pltpu.make_async_remote_copy(
                src_ref=src, dst_ref=dst, send_sem=send, recv_sem=recv,
                device_id=target, device_id_type=MESH,
            ).start()

    def sent(src, send, own):
        @pl.when(jnp.logical_not(own))
        def _():
            wait_for(src, send)

    w_home = [inverse.at[0, :, pl.ds(FIRST[p], PARTS[p])] for p in range(2)]
    a_home = acts.at[0]
    for p in range(2):
        deliver(
            w_home[p], w_ring[p].at[z, pl.ds(0, ROWS)], swap_send.at[8 * p],
            swap_recv.at[8 * p], at(side, core, z), same,
        )
    own_rows = pl.ds(pl.multiple_of(side * ROWS, 16), ROWS)
    for q in range(2):
        deliver(
            a_home, a_own.at[own_rows], swap_send.at[1 + q], swap_recv.at[1 + side],
            at(q, core, z), jnp.logical_and(same, core == q),
        )

    damp_out[...] = jnp.full((8, 128), damping[0], jnp.float32)

    @pl.when(same)
    def _():
        damp_in[...] = damp_out[...]
        pltpu.make_async_remote_copy(
            src_ref=damp_out, dst_ref=damp_in, send_sem=swap_send.at[7],
            recv_sem=swap_recv.at[7], device_id=sibling, device_id_type=MESH,
        ).start()

    def send_panel(src, dst, first):
        for q in range(2):
            deliver(
                src.at[q], dst.at[:, own_rows], swap_send.at[first + q],
                swap_recv.at[first + side],
                at(q, core, z), jnp.logical_and(same, core == q),
            )

    rings = [a_ring[0], a_ring[1], w_ring[0], w_ring[1]]
    streams_of = []
    for p in range(2):
        streams_of.append(range(len(rings), len(rings) + len(STREAMS[p])))
        rings += [x_ring[p][q] for q in range(len(STREAMS[p]))]

    def ring_ref(stream, place):
        return rings[stream].at[place, pl.ds(0, ROWS)]

    def far(stream):
        return (HOPS, HOPS - 1) if stream in LONG_UP else (HOPS - 1, HOPS)

    def place_of(way, hop):
        return (z - hop + NZ) % NZ if way == 0 else (z + hop) % NZ

    def step(stream, hop):
        for way in range(2):
            if hop <= far(stream)[way]:
                place = place_of(way, hop)
                ref = ring_ref(stream, place)
                if hop > 0:
                    wait_for(ref, ring_recv.at[stream, place])
                if hop < far(stream)[way]:
                    pltpu.make_async_remote_copy(
                        src_ref=ref, dst_ref=ref, send_sem=ring_send.at[stream, way, hop],
                        recv_sem=ring_recv.at[stream, place],
                        device_id=up if way == 0 else down, device_id_type=MESH,
                    ).start()
                    pending.append(
                        lambda r=ref, m=ring_send.at[stream, way, hop]: wait_for(r, m)
                    )

    def damp_block(place):
        outer = sum(
            lax.dot_general(
                a_own[:, FIRST[p] : FIRST[p] + PARTS[p]], a_ring[p][place],
                (((1,), (1,)), ((), ())), preferred_element_type=jnp.float32,
            )
            for p in range(2)
        )
        damped = BETA * f_work[place].astype(jnp.float32) + ((1.0 - BETA) / TOK) * outer
        f_work[place] = damped.astype(jnp.bfloat16)

    def first_product(p):
        def product(place):
            total[p][...] += jnp.dot(
                f_work[place], w_ring[p][place], preferred_element_type=jnp.float32
            )
        return product

    def second_product(p):
        def product(place):
            first = 0
            for q, width in enumerate(STREAMS[p]):
                total[p][:, first : first + width] += jnp.dot(
                    p_work[place], x_ring[p][q][place], preferred_element_type=jnp.float32
                )
                first += width
        return product

    def both(product, hop):
        if hop == 0:
            product(z)
        elif hop == HOPS:
            product((z + HOPS) % NZ)
        else:
            def one(s, carry):
                product((z + NZ + (1 - 2 * s) * hop) % NZ)
                return carry
            lax.fori_loop(0, 2, one, 0)

    mine = pl.ds(pl.multiple_of(core * ROWS, 16), ROWS)
    other = pl.ds(pl.multiple_of((1 - core) * ROWS, 16), ROWS)

    def pair_copy(p, phase):
        return pltpu.make_async_remote_copy(
            src_ref=total[p].at[other], dst_ref=sibling_part[p].at[phase],
            send_sem=pair_send.at[p, phase], recv_sem=pair_recv.at[p, phase],
            device_id=sibling, device_id_type=MESH,
        )

    for p in range(2):
        wait_for(w_ring[p].at[z, pl.ds(0, ROWS)], swap_recv.at[8 * p])
        step(2 + p, 0)
    wait_for(a_own.at[mine], swap_recv.at[1 + core])
    first = 0
    for p in range(2):
        a_ring[p][z, 0:ROWS, :] = a_own[mine, first : first + PARTS[p]]
        first += PARTS[p]
        step(p, 0)
    f_load.wait()
    relayout(f_in, f_out)
    wait_for(a_own.at[other], swap_recv.at[2 - core])
    send_panel(f_out, f_work, 3)
    p_load.wait()
    owner_load.wait()
    relayout(p_in, p_out)
    for p in range(2):
        total[p][...] = jnp.zeros_like(total[p])

    done = [0, 0]

    def catch_up(p, hop):
        for _ in range(2):
            if done[p] <= hop:
                if p == 0:
                    both(damp_block, done[p])
                both(first_product(p), done[p])
                done[p] += 1

    for hop in range(1, HOPS + 1):
        for stream in range(3):
            step(stream, hop)
        if hop < HOPS:
            step(3, hop)
        if hop in (2, 4, 6):
            greeted(hop // 2 - 1)
            if hop < 6:
                greet(hop // 2)
        if hop == 4:
            for b in range(2):
                wait_for(f_work.at[:, pl.ds(b * ROWS, ROWS)], swap_recv.at[3 + b])
            send_panel(p_out, p_work, 5)
        if hop >= 4:
            catch_up(0, hop)
            if hop == HOPS:
                pair_copy(0, 0).start()
                step(3, hop)
            catch_up(1, hop)

    @pl.when(jnp.logical_not(same))
    def _():
        wait_for(damp_in, swap_recv.at[7])

    def apply(p):
        pair_copy(p, 0).wait()
        window = w_ring[p][z, 0:ROWS, :].astype(jnp.float32)
        applied = total[p][mine, :] + sibling_part[p][0] + damp_in[0:1, 0:1] * window
        applied = applied.astype(jnp.bfloat16)
        first = 0
        for q, width in enumerate(STREAMS[p]):
            x_ring[p][q][z, 0:ROWS, :] = applied[:, first : first + width]
            step(streams_of[p][q], 0)
            first += width
        total[p][...] = jnp.zeros_like(total[p])

    pair_copy(1, 0).start()
    apply(0)
    apply(1)
    for b in range(2):
        wait_for(p_work.at[:, pl.ds(b * ROWS, ROWS)], swap_recv.at[5 + b])
    for p in range(2):
        both(second_product(p), 0)
    for hop in range(1, HOPS + 1):
        for p in range(2):
            for stream in streams_of[p]:
                step(stream, hop)
            both(second_product(p), hop)
            if hop == HOPS:
                pair_copy(p, 1).start()

    layer = chip * 2 + side
    for p in range(2):
        pair_copy(p, 1).wait()
        window = w_ring[p][z, 0:ROWS, :].astype(jnp.float32)
        fresh[p][...] = (
            2.0 * window - (total[p][mine, :] + sibling_part[p][1])
        ).astype(jnp.bfloat16)
        for r in range(PIECES):
            target = 2 * r + r % 2
            deliver(
                fresh[p].at[pl.ds(r * 16, 16)], gathered[p].at[layer],
                give_send.at[p, r], give_recv.at[p, layer], (target, z * 2 + core),
                jnp.logical_and(slot == target, side == core),
            )

    piece = chip
    middle = jnp.logical_and(chip < PIECES, core == chip % 2)
    piece_rows = pl.ds(pl.multiple_of((chip % PIECES) * 16, 16), 16)

    @pl.when(middle)
    def _():
        for p in range(2):
            for s in range(NS):
                wait_for(gathered[p].at[s], give_recv.at[p, s])
            for l in range(NS):
                picked[p][l * 16 : (l + 1) * 16, :] = gathered[p][owner[l]]
                deliver(
                    picked[p].at[pl.ds(l * 16, 16)],
                    out.at[0, piece_rows, pl.ds(FIRST[p], PARTS[p])],
                    pick_send.at[p, l], pick_recv.at[p, piece], (l, blk), slot == l,
                )
                pending.pop()

    for left in pending:
        left()

    @pl.when(same)
    def _():
        wait_for(damp_out, swap_send.at[7])

    @pl.when(middle)
    def _():
        for p in range(2):
            for l in range(NS):
                sent(picked[p].at[pl.ds(l * 16, 16)], pick_send.at[p, l], slot == l)

    for p in range(2):
        for r in range(PIECES):
            wait_for(
                out.at[0, pl.ds(r * 16, 16), pl.ds(FIRST[p], PARTS[p])], pick_recv.at[p, r]
            )


def shards(owner, factor, inverse_old, acts_t, damping):
    bf16, f32 = jnp.bfloat16, jnp.float32
    dma, vmem = pltpu.SemaphoreType.DMA, pltpu.VMEM
    n_streams = 4 + sum(len(widths) for widths in STREAMS)
    width = factor.shape[2]
    smem = pl.BlockSpec(memory_space=pltpu.SMEM)
    anywhere = pl.BlockSpec(memory_space=pltpu.HBM)
    return pl.pallas_call(
        kernel,
        out_shape=jax.ShapeDtypeStruct((1, ROWS, COLS), bf16),
        in_specs=[anywhere, smem, anywhere, anywhere, anywhere],
        out_specs=pl.BlockSpec(memory_space=pltpu.VMEM),
        scratch_shapes=[
            pltpu.SMEM((NS,), jnp.int32),
            vmem((ROWS, width), f32),
            vmem((ROWS, width), bf16),
            vmem((2, NZ, ROWS, KP), bf16),
            vmem((2, NZ, ROWS, KP), bf16),
            vmem((NZ, 2 * ROWS, KP), bf16),
            vmem((NZ, 2 * ROWS, KP), bf16),
            vmem((2 * ROWS, TOK), bf16),
            [vmem((NZ, KP, n), bf16) for n in PARTS],
            [vmem((NZ, KP, n), bf16) for n in PARTS],
            [[vmem((NZ, KP, n), bf16) for n in widths] for widths in STREAMS],
            [vmem((2 * ROWS, n), f32) for n in PARTS],
            [vmem((2, ROWS, n), f32) for n in PARTS],
            [vmem((ROWS, n), bf16) for n in PARTS],
            [vmem((NS, 16, n), bf16) for n in PARTS],
            [vmem((NS * 16, n), bf16) for n in PARTS],
            vmem((8, 128), f32),
            vmem((8, 128), f32),
            dma((3,)),
            dma((9,)),
            dma((9,)),
            dma((n_streams, 2, HOPS)),
            dma((n_streams, NZ)),
            dma((2, 2)),
            dma((2, 2)),
            dma((2, PIECES)),
            dma((2, NS)),
            dma((2, NS)),
            dma((2, PIECES)),
            pltpu.SemaphoreType.REGULAR((3,)),
        ],
        compiler_params=pltpu.CompilerParams(
            collective_id=0, has_side_effects=True, vmem_limit_bytes=60 * 1024 * 1024
        ),
        cost_estimate=pl.CostEstimate(
            flops=2 * 3 * ROWS * width * COLS, bytes_accessed=3 * 1024 * 1024, transcendentals=0
        ),
    )(owner, damping, factor, inverse_old, acts_t)


def solution(mesh):
    placed = (
        P(),
        P("slot", "blk", None),
        P("slot", "blk", None),
        P("slot", "blk", None),
        P("slot"),
    )
    return jax.shard_map(
        shards, mesh=mesh, in_specs=placed, out_specs=P("slot", "blk", None), check_vma=False
    )
```

```python
import jax
import jax.numpy as jnp
from jax import lax
from jax.experimental import pallas as pl
from jax.experimental.pallas import tpu as pltpu
from jax.sharding import PartitionSpec as P

COLS = 640
TOK = 640
BETA = 0.75
NZ = 16
NS = 16
ROWS = 112
KP = 128
PIECES = 7
MESH = pl.DeviceIdType.MESH
HOPS = NZ // 2
PARTS = (256, 384)
FIRST = (0, 256)
STREAMS = ((128, 128), (128, 128, 128))
LONG_UP = (0, 3, 4, 6, 8)


def wait_for(ref, sem):
    pltpu.make_async_copy(ref, ref, sem).wait()


def kernel(
    owner_home, damping, factor, inverse, acts, out,
    owner, f_in, p_in, f_out, p_out, f_work, p_work, a_own, a_ring,
    w_ring, x_ring, total, sibling_part, fresh, gathered, picked,
    damp_out, damp_in, load_sem,
    swap_send, swap_recv, ring_send, ring_recv, pair_send, pair_recv,
    give_send, give_recv, pick_send, pick_recv, hello,
):
    slot = lax.axis_index("slot")
    blk = lax.axis_index("blk")
    chip = slot // 2
    core = slot % 2
    z = blk // 2
    side = blk % 2
    same = core == side

    def at(core_at, side_at, z_at):
        return (chip * 2 + core_at, z_at * 2 + side_at)

    sibling = at(1 - core, side, z)
    up = at(core, side, (z + 1) % NZ)
    down = at(core, side, (z + NZ - 1) % NZ)

    barrier = pltpu.get_barrier_semaphore()
    def other_chip(c, side_at):
        return (c * 2 + core, z * 2 + side_at)

    along_x = chip // 4 * 4
    far_partners = [
        other_chip((chip + 4) % 8, 1 - side),
        other_chip(along_x + chip % 4 // 2 * 2 + 1 - chip % 2, side),
        other_chip(along_x + 3 - chip % 4, side),
    ]
    partners = [up, down, sibling, at(core, 1 - side, z), at(1 - core, 1 - side, z)]
    for target in partners + far_partners:
        pl.semaphore_signal(barrier, inc=1, device_id=target, device_id_type=MESH)

    f_load = pltpu.make_async_copy(factor.at[0], f_in, load_sem.at[0])
    p_load = pltpu.make_async_copy(inverse.at[0], p_in, load_sem.at[1])
    f_load.start()
    p_load.start()
    owner_load = pltpu.make_async_copy(owner_home, owner, load_sem.at[2])
    owner_load.start()

    def greet(i):
        pl.semaphore_signal(
            hello.at[i], inc=1, device_id=far_partners[i], device_id_type=MESH
        )

    def greeted(i):
        pl.semaphore_wait(hello.at[i], 1)

    pending = []

    def keep(src, dst, recv, own):
        @pl.when(own)
        def _():
            pltpu.make_async_copy(src, dst, recv).start()

    def deliver(src, dst, send, recv, target, own, kept=False):
        pending.append(lambda: sent(src, send, own))

        if not kept:
            keep(src, dst, recv, own)

        @pl.when(jnp.logical_not(own))
        def _():
            pltpu.make_async_remote_copy(
                src_ref=src, dst_ref=dst, send_sem=send, recv_sem=recv,
                device_id=target, device_id_type=MESH,
            ).start()

    def sent(src, send, own):
        @pl.when(jnp.logical_not(own))
        def _():
            wait_for(src, send)

    w_home = [inverse.at[0, :, pl.ds(FIRST[p], PARTS[p])] for p in range(2)]
    a_home = acts.at[0]
    own_rows = pl.ds(pl.multiple_of(side * ROWS, 16), ROWS)

    for p in range(2):
        keep(w_home[p], w_ring[p].at[z, pl.ds(0, ROWS)], swap_recv.at[8 * p], same)
    keep(a_home, a_own.at[own_rows], swap_recv.at[1 + side], same)

    pad = jnp.zeros((KP - ROWS, COLS), jnp.bfloat16)

    def clear(i, carry):
        for p in range(2):
            a_ring[p][i, ROWS:KP, :] = pad[:, : PARTS[p]]
            w_ring[p][i, ROWS:KP, :] = pad[:, : PARTS[p]]
            for q, width in enumerate(STREAMS[p]):
                x_ring[p][q][i, ROWS:KP, :] = pad[:, :width]
        return carry

    lax.fori_loop(0, NZ, clear, 0)
    def relayout(src, dst):
        for j in range(2 * NZ):
            start = ROWS * j
            base = start // 128 * 128
            off = start - base
            if off == 0:
                piece = src[:, base : base + 128].astype(jnp.bfloat16)
            elif off + ROWS <= 128:
                piece = pltpu.roll(
                    src[:, base : base + 128].astype(jnp.float32), 128 - off, 1
                ).astype(jnp.bfloat16)
            else:
                piece = pltpu.roll(
                    src[:, base : base + 256].astype(jnp.float32), 256 - off, 1
                )[:, :128].astype(jnp.bfloat16)
            dst[j % 2, j // 2] = piece

    pl.semaphore_wait(barrier, len(partners) + len(far_partners))
    greet(0)

    def swap_w(p):
        deliver(
            w_home[p], w_ring[p].at[z, pl.ds(0, ROWS)], swap_send.at[8 * p],
            swap_recv.at[8 * p], at(side, core, z), same, True,
        )

    def swap_a(q, own):
        deliver(
            a_home, a_own.at[own_rows], swap_send.at[1 + q], swap_recv.at[1 + side],
            at(side if q == 0 else 1 - side, core, z), own, True,
        )

    swap_w(0)
    swap_a(0, same)
    swap_w(1)
    swap_a(1, False)

    damp_out[...] = jnp.full((8, 128), damping[0], jnp.float32)

    @pl.when(same)
    def _():
        damp_in[...] = damp_out[...]
        pltpu.make_async_remote_copy(
            src_ref=damp_out, dst_ref=damp_in, send_sem=swap_send.at[7],
            recv_sem=swap_recv.at[7], device_id=sibling, device_id_type=MESH,
        ).start()

    def send_panel(src, dst, first):
        for q in range(2):
            deliver(
                src.at[q], dst.at[:, own_rows], swap_send.at[first + q],
                swap_recv.at[first + side],
                at(q, core, z), jnp.logical_and(same, core == q),
            )

    rings = [a_ring[0], a_ring[1], w_ring[0], w_ring[1]]
    streams_of = []
    for p in range(2):
        streams_of.append(range(len(rings), len(rings) + len(STREAMS[p])))
        rings += [x_ring[p][q] for q in range(len(STREAMS[p]))]

    def ring_ref(stream, place):
        return rings[stream].at[place, pl.ds(0, ROWS)]

    def far(stream):
        return (HOPS, HOPS - 1) if stream in LONG_UP else (HOPS - 1, HOPS)

    def place_of(way, hop):
        return (z - hop + NZ) % NZ if way == 0 else (z + hop) % NZ

    def step(stream, hop):
        for way in range(2):
            if hop <= far(stream)[way]:
                place = place_of(way, hop)
                ref = ring_ref(stream, place)
                if hop > 0:
                    wait_for(ref, ring_recv.at[stream, place])
                if hop < far(stream)[way]:
                    pltpu.make_async_remote_copy(
                        src_ref=ref, dst_ref=ref, send_sem=ring_send.at[stream, way, hop],
                        recv_sem=ring_recv.at[stream, place],
                        device_id=up if way == 0 else down, device_id_type=MESH,
                    ).start()
                    pending.append(
                        lambda r=ref, m=ring_send.at[stream, way, hop]: wait_for(r, m)
                    )

    def damp_block(place):
        outer = sum(
            lax.dot_general(
                a_own[:, FIRST[p] : FIRST[p] + PARTS[p]], a_ring[p][place],
                (((1,), (1,)), ((), ())), preferred_element_type=jnp.float32,
            )
            for p in range(2)
        )
        damped = BETA * f_work[place].astype(jnp.float32) + ((1.0 - BETA) / TOK) * outer
        f_work[place] = damped.astype(jnp.bfloat16)

    def first_product(p):
        def product(place):
            total[p][...] += jnp.dot(
                f_work[place], w_ring[p][place], preferred_element_type=jnp.float32
            )
        return product

    def second_product(p):
        def product(place):
            first = 0
            for q, width in enumerate(STREAMS[p]):
                total[p][:, first : first + width] += jnp.dot(
                    p_work[place], x_ring[p][q][place], preferred_element_type=jnp.float32
                )
                first += width
        return product

    def both(product, hop):
        if hop == 0:
            product(z)
        elif hop == HOPS:
            product((z + HOPS) % NZ)
        else:
            def one(s, carry):
                product((z + NZ + (1 - 2 * s) * hop) % NZ)
                return carry
            lax.fori_loop(0, 2, one, 0)

    mine = pl.ds(pl.multiple_of(core * ROWS, 16), ROWS)
    other = pl.ds(pl.multiple_of((1 - core) * ROWS, 16), ROWS)

    def pair_copy(p, phase):
        return pltpu.make_async_remote_copy(
            src_ref=total[p].at[other], dst_ref=sibling_part[p].at[phase],
            send_sem=pair_send.at[p, phase], recv_sem=pair_recv.at[p, phase],
            device_id=sibling, device_id_type=MESH,
        )

    wait_for(w_ring[0].at[z, pl.ds(0, ROWS)], swap_recv.at[0])
    step(2, 0)
    wait_for(a_own.at[mine], swap_recv.at[1 + core])
    first = 0
    for p in range(2):
        a_ring[p][z, 0:ROWS, :] = a_own[mine, first : first + PARTS[p]]
        first += PARTS[p]
        step(p, 0)
    wait_for(w_ring[1].at[z, pl.ds(0, ROWS)], swap_recv.at[8])
    step(3, 0)
    f_load.wait()
    relayout(f_in, f_out)
    wait_for(a_own.at[other], swap_recv.at[2 - core])
    send_panel(f_out, f_work, 3)
    p_load.wait()
    owner_load.wait()
    relayout(p_in, p_out)
    for p in range(2):
        total[p][...] = jnp.zeros_like(total[p])

    done = [0, 0]

    def catch_up(p, hop):
        for _ in range(2):
            if done[p] <= hop:
                if p == 0:
                    both(damp_block, done[p])
                both(first_product(p), done[p])
                done[p] += 1

    for hop in range(1, HOPS + 1):
        for stream in (2, 0, 1):
            step(stream, hop)
        if hop < HOPS:
            step(3, hop)
        if hop in (2, 4, 6):
            greeted(hop // 2 - 1)
            if hop < 6:
                greet(hop // 2)
        if hop == 4:
            for b in range(2):
                wait_for(f_work.at[:, pl.ds(b * ROWS, ROWS)], swap_recv.at[3 + b])
            send_panel(p_out, p_work, 5)
        if hop >= 4:
            catch_up(0, hop)
            if hop == HOPS:
                pair_copy(0, 0).start()
                step(3, hop)
            catch_up(1, hop)

    @pl.when(jnp.logical_not(same))
    def _():
        wait_for(damp_in, swap_recv.at[7])

    def apply(p):
        pair_copy(p, 0).wait()
        window = w_ring[p][z, 0:ROWS, :].astype(jnp.float32)
        applied = total[p][mine, :] + sibling_part[p][0] + damp_in[0:1, 0:1] * window
        applied = applied.astype(jnp.bfloat16)
        first = 0
        for q, width in enumerate(STREAMS[p]):
            x_ring[p][q][z, 0:ROWS, :] = applied[:, first : first + width]
            step(streams_of[p][q], 0)
            first += width
        total[p][...] = jnp.zeros_like(total[p])

    pair_copy(1, 0).start()
    apply(0)
    apply(1)
    for b in range(2):
        wait_for(p_work.at[:, pl.ds(b * ROWS, ROWS)], swap_recv.at[5 + b])
    for p in range(2):
        both(second_product(p), 0)
    for hop in range(1, HOPS + 1):
        for p in range(2):
            for stream in streams_of[p]:
                step(stream, hop)
            if hop == HOPS:
                both(second_product(p), hop)
                pair_copy(p, 1).start()
        if hop < HOPS:
            for p in range(2):
                both(second_product(p), hop)

    layer = chip * 2 + side
    for p in range(2):
        pair_copy(p, 1).wait()
        window = w_ring[p][z, 0:ROWS, :].astype(jnp.float32)
        fresh[p][...] = (
            2.0 * window - (total[p][mine, :] + sibling_part[p][1])
        ).astype(jnp.bfloat16)
        for r in range(PIECES):
            target = 2 * r + p
            deliver(
                fresh[p].at[pl.ds(r * 16, 16)], gathered[p].at[layer],
                give_send.at[p, r], give_recv.at[p, layer], (target, z * 2 + core),
                jnp.logical_and(slot == target, side == core),
            )

    def middle(p):
        return jnp.logical_and(chip < PIECES, core == p)

    piece_rows = pl.ds(pl.multiple_of((chip % PIECES) * 16, 16), 16)
    for p in range(2):
        @pl.when(middle(p))
        def _():
            for layer_at in range(NS):
                wait_for(gathered[p].at[layer_at], give_recv.at[p, layer_at])
            for l in range(NS):
                picked[p][l * 16 : (l + 1) * 16, :] = gathered[p][owner[l]]
                deliver(
                    picked[p].at[pl.ds(l * 16, 16)],
                    out.at[0, piece_rows, pl.ds(FIRST[p], PARTS[p])],
                    pick_send.at[p, l], pick_recv.at[p, chip], (l, blk), slot == l,
                )
                pending.pop()

    for left in pending:
        left()

    @pl.when(same)
    def _():
        wait_for(damp_out, swap_send.at[7])

    for p in range(2):
        @pl.when(middle(p))
        def _():
            for l in range(NS):
                sent(picked[p].at[pl.ds(l * 16, 16)], pick_send.at[p, l], slot == l)

    for p in range(2):
        for r in range(PIECES):
            wait_for(
                out.at[0, pl.ds(r * 16, 16), pl.ds(FIRST[p], PARTS[p])], pick_recv.at[p, r]
            )


def shards(owner, factor, inverse_old, acts_t, damping):
    bf16, f32 = jnp.bfloat16, jnp.float32
    dma, vmem = pltpu.SemaphoreType.DMA, pltpu.VMEM
    n_streams = 4 + sum(len(widths) for widths in STREAMS)
    width = factor.shape[2]
    smem = pl.BlockSpec(memory_space=pltpu.SMEM)
    anywhere = pl.BlockSpec(memory_space=pltpu.HBM)
    return pl.pallas_call(
        kernel,
        out_shape=jax.ShapeDtypeStruct((1, ROWS, COLS), bf16),
        in_specs=[anywhere, smem, anywhere, anywhere, anywhere],
        out_specs=anywhere,
        scratch_shapes=[
            pltpu.SMEM((NS,), jnp.int32),
            vmem((ROWS, width), f32),
            vmem((ROWS, width), bf16),
            vmem((2, NZ, ROWS, KP), bf16),
            vmem((2, NZ, ROWS, KP), bf16),
            vmem((NZ, 2 * ROWS, KP), bf16),
            vmem((NZ, 2 * ROWS, KP), bf16),
            vmem((2 * ROWS, TOK), bf16),
            [vmem((NZ, KP, n), bf16) for n in PARTS],
            [vmem((NZ, KP, n), bf16) for n in PARTS],
            [[vmem((NZ, KP, n), bf16) for n in widths] for widths in STREAMS],
            [vmem((2 * ROWS, n), f32) for n in PARTS],
            [vmem((2, ROWS, n), f32) for n in PARTS],
            [vmem((ROWS, n), bf16) for n in PARTS],
            [vmem((NS, 16, n), bf16) for n in PARTS],
            [vmem((NS * 16, n), bf16) for n in PARTS],
            vmem((8, 128), f32),
            vmem((8, 128), f32),
            dma((3,)),
            dma((9,)),
            dma((9,)),
            dma((n_streams, 2, HOPS)),
            dma((n_streams, NZ)),
            dma((2, 2)),
            dma((2, 2)),
            dma((2, PIECES)),
            dma((2, NS)),
            dma((2, NS)),
            dma((2, PIECES)),
            pltpu.SemaphoreType.REGULAR((3,)),
        ],
        compiler_params=pltpu.CompilerParams(
            collective_id=0, has_side_effects=True, vmem_limit_bytes=60 * 1024 * 1024
        ),
        cost_estimate=pl.CostEstimate(
            flops=2 * 3 * ROWS * width * COLS, bytes_accessed=3 * 1024 * 1024, transcendentals=0
        ),
    )(owner, damping, factor, inverse_old, acts_t)


def solution(mesh):
    placed = (
        P(),
        P("slot", "blk", None),
        P("slot", "blk", None),
        P("slot", "blk", None),
        P("slot"),
    )
    return jax.shard_map(
        shards, mesh=mesh, in_specs=placed, out_specs=P("slot", "blk", None), check_vma=False
    )
```

```python
import jax
import jax.numpy as jnp
from jax import lax
from jax.experimental import pallas as pl
from jax.experimental.pallas import tpu as pltpu
from jax.sharding import PartitionSpec as P

COLS = 640
TOK = 640
BETA = 0.75
NZ = 16
NS = 16
ROWS = 112
KP = 128
PIECES = 7
MESH = pl.DeviceIdType.MESH
HOPS = NZ // 2
PARTS = (256, 384)
FIRST = (0, 256)
STREAMS = ((128, 128), (128, 128, 128))
LONG_UP = (0, 3, 4, 6, 8)


def wait_for(ref, sem):
    pltpu.make_async_copy(ref, ref, sem).wait()


def kernel(
    owner_home, damping, factor, inverse, acts, out,
    owner, f_in, p_in, f_out, p_out, f_work, p_work, a_own, a_ring,
    w_ring, x_ring, total, sibling_part, fresh, gathered, picked,
    damp_out, damp_in, load_sem,
    swap_send, swap_recv, ring_send, ring_recv, pair_send, pair_recv,
    give_send, give_recv, pick_send, pick_recv, hello,
):
    slot = lax.axis_index("slot")
    blk = lax.axis_index("blk")
    chip = slot // 2
    core = slot % 2
    z = blk // 2
    side = blk % 2
    same = core == side

    def at(core_at, side_at, z_at):
        return (chip * 2 + core_at, z_at * 2 + side_at)

    sibling = at(1 - core, side, z)
    up = at(core, side, (z + 1) % NZ)
    down = at(core, side, (z + NZ - 1) % NZ)

    barrier = pltpu.get_barrier_semaphore()
    def other_chip(c, side_at):
        return (c * 2 + core, z * 2 + side_at)

    along_x = chip // 4 * 4
    far_partners = [
        other_chip((chip + 4) % 8, 1 - side),
        other_chip(along_x + chip % 4 // 2 * 2 + 1 - chip % 2, side),
        other_chip(along_x + 3 - chip % 4, side),
    ]
    partners = [up, down, sibling, at(core, 1 - side, z), at(1 - core, 1 - side, z)]
    swap_up = at(side, core, (z + 1) % NZ)
    swap_down = at(side, core, (z + NZ - 1) % NZ)

    @pl.when(jnp.logical_not(same))
    def _():
        for target in (swap_up, swap_down):
            pl.semaphore_signal(barrier, inc=1, device_id=target, device_id_type=MESH)

    for target in partners + far_partners:
        pl.semaphore_signal(barrier, inc=1, device_id=target, device_id_type=MESH)

    f_load = pltpu.make_async_copy(factor.at[0], f_in, load_sem.at[0])
    p_load = pltpu.make_async_copy(inverse.at[0], p_in, load_sem.at[1])
    f_load.start()
    p_load.start()
    owner_load = pltpu.make_async_copy(owner_home, owner, load_sem.at[2])
    owner_load.start()

    def greet(i):
        pl.semaphore_signal(
            hello.at[i], inc=1, device_id=far_partners[i], device_id_type=MESH
        )

    def greeted(i):
        pl.semaphore_wait(hello.at[i], 1)

    pending = []

    def keep(src, dst, recv, own):
        @pl.when(own)
        def _():
            pltpu.make_async_copy(src, dst, recv).start()

    def deliver(src, dst, send, recv, target, own, kept=False):
        pending.append(lambda: sent(src, send, own))

        if not kept:
            keep(src, dst, recv, own)

        @pl.when(jnp.logical_not(own))
        def _():
            pltpu.make_async_remote_copy(
                src_ref=src, dst_ref=dst, send_sem=send, recv_sem=recv,
                device_id=target, device_id_type=MESH,
            ).start()

    def sent(src, send, own):
        @pl.when(jnp.logical_not(own))
        def _():
            wait_for(src, send)

    w_home = [inverse.at[0, :, pl.ds(FIRST[p], PARTS[p])] for p in range(2)]
    a_home = acts.at[0]
    own_rows = pl.ds(pl.multiple_of(side * ROWS, 16), ROWS)

    for p in range(2):
        keep(w_home[p], w_ring[p].at[z, pl.ds(0, ROWS)], swap_recv.at[8 * p], same)
    keep(a_home, a_own.at[own_rows], swap_recv.at[1 + side], same)

    pad = jnp.zeros((KP - ROWS, COLS), jnp.bfloat16)

    def clear(i, carry):
        for p in range(2):
            a_ring[p][i, ROWS:KP, :] = pad[:, : PARTS[p]]
            w_ring[p][i, ROWS:KP, :] = pad[:, : PARTS[p]]
            for q, width in enumerate(STREAMS[p]):
                x_ring[p][q][i, ROWS:KP, :] = pad[:, :width]
        return carry

    lax.fori_loop(0, NZ, clear, 0)
    def relayout(src, dst):
        for j in range(2 * NZ):
            start = ROWS * j
            base = start // 128 * 128
            off = start - base
            if off == 0:
                piece = src[:, base : base + 128].astype(jnp.bfloat16)
            elif off + ROWS <= 128:
                piece = pltpu.roll(
                    src[:, base : base + 128].astype(jnp.float32), 128 - off, 1
                ).astype(jnp.bfloat16)
            else:
                piece = pltpu.roll(
                    src[:, base : base + 256].astype(jnp.float32), 256 - off, 1
                )[:, :128].astype(jnp.bfloat16)
            dst[j % 2, j // 2] = piece

    @pl.when(same)
    def _():
        pl.semaphore_wait(barrier, len(partners) + len(far_partners))

    @pl.when(jnp.logical_not(same))
    def _():
        pl.semaphore_wait(barrier, len(partners) + len(far_partners) + 2)

    greet(0)

    def swap_w(p):
        deliver(
            w_home[p], w_ring[p].at[z, pl.ds(0, ROWS)], swap_send.at[8 * p],
            swap_recv.at[8 * p], at(side, core, z), same, True,
        )

    def swap_a(q, own):
        deliver(
            a_home, a_own.at[own_rows], swap_send.at[1 + q], swap_recv.at[1 + side],
            at(side if q == 0 else 1 - side, core, z), own, True,
        )

    rings = [a_ring[0], a_ring[1], w_ring[0], w_ring[1]]
    streams_of = []
    for p in range(2):
        streams_of.append(range(len(rings), len(rings) + len(STREAMS[p])))
        rings += [x_ring[p][q] for q in range(len(STREAMS[p]))]

    def ring_ref(stream, place):
        return rings[stream].at[place, pl.ds(0, ROWS)]

    def far(stream):
        return (HOPS, HOPS - 1) if stream in LONG_UP else (HOPS - 1, HOPS)

    def place_of(way, hop):
        return (z - hop + NZ) % NZ if way == 0 else (z + hop) % NZ

    def first_hop(stream):
        p = stream % 2
        home = w_home[p] if stream >= 2 else a_home.at[:, pl.ds(FIRST[p], PARTS[p])]
        for way in range(2):
            pltpu.make_async_remote_copy(
                src_ref=home, dst_ref=ring_ref(stream, z),
                send_sem=ring_send.at[stream, way, 0], recv_sem=ring_recv.at[stream, z],
                device_id=swap_up if way == 0 else swap_down, device_id_type=MESH,
            ).start()
            pending.append(lambda r=home, m=ring_send.at[stream, way, 0]: wait_for(r, m))

    first_hop(2)
    first_hop(0)
    first_hop(1)
    first_hop(3)
    swap_w(0)
    swap_a(0, same)
    swap_w(1)
    swap_a(1, False)

    damp_out[...] = jnp.full((8, 128), damping[0], jnp.float32)

    @pl.when(same)
    def _():
        damp_in[...] = damp_out[...]
        pltpu.make_async_remote_copy(
            src_ref=damp_out, dst_ref=damp_in, send_sem=swap_send.at[7],
            recv_sem=swap_recv.at[7], device_id=sibling, device_id_type=MESH,
        ).start()

    def send_panel(src, dst, first):
        for q in range(2):
            deliver(
                src.at[q], dst.at[:, own_rows], swap_send.at[first + q],
                swap_recv.at[first + side],
                at(q, core, z), jnp.logical_and(same, core == q),
            )

    def step(stream, hop):
        for way in range(2):
            if hop <= far(stream)[way]:
                place = place_of(way, hop)
                ref = ring_ref(stream, place)
                if hop > 0:
                    wait_for(ref, ring_recv.at[stream, place])
                if hop < far(stream)[way]:
                    pltpu.make_async_remote_copy(
                        src_ref=ref, dst_ref=ref, send_sem=ring_send.at[stream, way, hop],
                        recv_sem=ring_recv.at[stream, place],
                        device_id=up if way == 0 else down, device_id_type=MESH,
                    ).start()
                    pending.append(
                        lambda r=ref, m=ring_send.at[stream, way, hop]: wait_for(r, m)
                    )

    def damp_block(place):
        outer = sum(
            lax.dot_general(
                a_own[:, FIRST[p] : FIRST[p] + PARTS[p]], a_ring[p][place],
                (((1,), (1,)), ((), ())), preferred_element_type=jnp.float32,
            )
            for p in range(2)
        )
        damped = BETA * f_work[place].astype(jnp.float32) + ((1.0 - BETA) / TOK) * outer
        f_work[place] = damped.astype(jnp.bfloat16)

    def first_product(p):
        def product(place):
            total[p][...] += jnp.dot(
                f_work[place], w_ring[p][place], preferred_element_type=jnp.float32
            )
        return product

    def second_product(p):
        def product(place):
            first = 0
            for q, width in enumerate(STREAMS[p]):
                total[p][:, first : first + width] += jnp.dot(
                    p_work[place], x_ring[p][q][place], preferred_element_type=jnp.float32
                )
                first += width
        return product

    def both(product, hop):
        if hop == 0:
            product(z)
        elif hop == HOPS:
            product((z + HOPS) % NZ)
        else:
            def one(s, carry):
                product((z + NZ + (1 - 2 * s) * hop) % NZ)
                return carry
            lax.fori_loop(0, 2, one, 0)

    mine = pl.ds(pl.multiple_of(core * ROWS, 16), ROWS)
    other = pl.ds(pl.multiple_of((1 - core) * ROWS, 16), ROWS)

    def pair_copy(p, phase):
        return pltpu.make_async_remote_copy(
            src_ref=total[p].at[other], dst_ref=sibling_part[p].at[phase],
            send_sem=pair_send.at[p, phase], recv_sem=pair_recv.at[p, phase],
            device_id=sibling, device_id_type=MESH,
        )

    f_load.wait()
    relayout(f_in, f_out)
    send_panel(f_out, f_work, 3)
    p_load.wait()
    owner_load.wait()
    relayout(p_in, p_out)
    for p in range(2):
        total[p][...] = jnp.zeros_like(total[p])

    done = [0, 0]

    def catch_up(p, hop):
        for _ in range(2):
            if done[p] <= hop:
                if p == 0:
                    both(damp_block, done[p])
                both(first_product(p), done[p])
                done[p] += 1

    for hop in range(1, HOPS + 1):
        for stream in (2, 0, 1):
            step(stream, hop)
        if hop < HOPS:
            step(3, hop)
        if hop in (2, 4, 6):
            greeted(hop // 2 - 1)
            if hop < 6:
                greet(hop // 2)
        if hop == 2:
            for p in range(2):
                wait_for(w_ring[p].at[z, pl.ds(0, ROWS)], swap_recv.at[8 * p])
            wait_for(a_own.at[mine], swap_recv.at[1 + core])
            for p in range(2):
                a_ring[p][z, 0:ROWS, :] = a_own[mine, FIRST[p] : FIRST[p] + PARTS[p]]
        if hop == 4:
            for b in range(2):
                wait_for(f_work.at[:, pl.ds(b * ROWS, ROWS)], swap_recv.at[3 + b])
            wait_for(a_own.at[other], swap_recv.at[2 - core])
            send_panel(p_out, p_work, 5)
        if hop >= 4:
            catch_up(0, hop)
            if hop == HOPS:
                pair_copy(0, 0).start()
                step(3, hop)
            catch_up(1, hop)

    @pl.when(jnp.logical_not(same))
    def _():
        wait_for(damp_in, swap_recv.at[7])

    def apply(p):
        pair_copy(p, 0).wait()
        window = w_ring[p][z, 0:ROWS, :].astype(jnp.float32)
        applied = total[p][mine, :] + sibling_part[p][0] + damp_in[0:1, 0:1] * window
        applied = applied.astype(jnp.bfloat16)
        first = 0
        for q, width in enumerate(STREAMS[p]):
            x_ring[p][q][z, 0:ROWS, :] = applied[:, first : first + width]
            step(streams_of[p][q], 0)
            first += width
        total[p][...] = jnp.zeros_like(total[p])

    pair_copy(1, 0).start()
    apply(0)
    apply(1)
    for b in range(2):
        wait_for(p_work.at[:, pl.ds(b * ROWS, ROWS)], swap_recv.at[5 + b])
    for p in range(2):
        both(second_product(p), 0)
    early, pending[:] = list(pending), []
    for hop in range(1, HOPS + 1):
        for p in range(2):
            for stream in streams_of[p]:
                step(stream, hop)
            if hop == HOPS:
                both(second_product(p), hop)
                pair_copy(p, 1).start()
        if hop < HOPS:
            for p in range(2):
                both(second_product(p), hop)
        for left in early[(hop - 1) * len(early) // 6 : hop * len(early) // 6]:
            left()

    layer = chip * 2 + side
    for p in range(2):
        pair_copy(p, 1).wait()
        window = w_ring[p][z, 0:ROWS, :].astype(jnp.float32)
        fresh[p][...] = (
            2.0 * window - (total[p][mine, :] + sibling_part[p][1])
        ).astype(jnp.bfloat16)
        for r in range(PIECES):
            target = 2 * r + p
            deliver(
                fresh[p].at[pl.ds(r * 16, 16)], gathered[p].at[layer],
                give_send.at[p, r], give_recv.at[p, layer], (target, z * 2 + core),
                jnp.logical_and(slot == target, side == core),
            )

    for left in pending[:-2 * PIECES]:
        left()
    pending[:] = pending[-2 * PIECES :]

    def middle(p):
        return jnp.logical_and(chip < PIECES, core == p)

    piece_rows = pl.ds(pl.multiple_of((chip % PIECES) * 16, 16), 16)
    for p in range(2):
        @pl.when(middle(p))
        def _():
            for layer_at in range(NS):
                wait_for(gathered[p].at[layer_at], give_recv.at[p, layer_at])
            for l in range(NS):
                picked[p][l * 16 : (l + 1) * 16, :] = gathered[p][owner[l]]
                deliver(
                    picked[p].at[pl.ds(l * 16, 16)],
                    out.at[0, piece_rows, pl.ds(FIRST[p], PARTS[p])],
                    pick_send.at[p, l], pick_recv.at[p, chip], (l, blk), slot == l,
                )
                pending.pop()

    for left in pending:
        left()

    @pl.when(same)
    def _():
        wait_for(damp_out, swap_send.at[7])

    for p in range(2):
        @pl.when(middle(p))
        def _():
            for l in range(NS):
                sent(picked[p].at[pl.ds(l * 16, 16)], pick_send.at[p, l], slot == l)

    for p in range(2):
        for r in range(PIECES):
            wait_for(
                out.at[0, pl.ds(r * 16, 16), pl.ds(FIRST[p], PARTS[p])], pick_recv.at[p, r]
            )


def shards(owner, factor, inverse_old, acts_t, damping):
    bf16, f32 = jnp.bfloat16, jnp.float32
    dma, vmem = pltpu.SemaphoreType.DMA, pltpu.VMEM
    n_streams = 4 + sum(len(widths) for widths in STREAMS)
    width = factor.shape[2]
    smem = pl.BlockSpec(memory_space=pltpu.SMEM)
    anywhere = pl.BlockSpec(memory_space=pltpu.HBM)
    return pl.pallas_call(
        kernel,
        out_shape=jax.ShapeDtypeStruct((1, ROWS, COLS), bf16),
        in_specs=[anywhere, smem, anywhere, anywhere, anywhere],
        out_specs=anywhere,
        scratch_shapes=[
            pltpu.SMEM((NS,), jnp.int32),
            vmem((ROWS, width), f32),
            vmem((ROWS, width), bf16),
            vmem((2, NZ, ROWS, KP), bf16),
            vmem((2, NZ, ROWS, KP), bf16),
            vmem((NZ, 2 * ROWS, KP), bf16),
            vmem((NZ, 2 * ROWS, KP), bf16),
            vmem((2 * ROWS, TOK), bf16),
            [vmem((NZ, KP, n), bf16) for n in PARTS],
            [vmem((NZ, KP, n), bf16) for n in PARTS],
            [[vmem((NZ, KP, n), bf16) for n in widths] for widths in STREAMS],
            [vmem((2 * ROWS, n), f32) for n in PARTS],
            [vmem((2, ROWS, n), f32) for n in PARTS],
            [vmem((ROWS, n), bf16) for n in PARTS],
            [vmem((NS, 16, n), bf16) for n in PARTS],
            [vmem((NS * 16, n), bf16) for n in PARTS],
            vmem((8, 128), f32),
            vmem((8, 128), f32),
            dma((3,)),
            dma((9,)),
            dma((9,)),
            dma((n_streams, 2, HOPS)),
            dma((n_streams, NZ)),
            dma((2, 2)),
            dma((2, 2)),
            dma((2, PIECES)),
            dma((2, NS)),
            dma((2, NS)),
            dma((2, PIECES)),
            pltpu.SemaphoreType.REGULAR((3,)),
        ],
        compiler_params=pltpu.CompilerParams(
            collective_id=0, has_side_effects=True, vmem_limit_bytes=60 * 1024 * 1024
        ),
        cost_estimate=pl.CostEstimate(
            flops=2 * 3 * ROWS * width * COLS, bytes_accessed=3 * 1024 * 1024, transcendentals=0
        ),
    )(owner, damping, factor, inverse_old, acts_t)


def solution(mesh):
    placed = (
        P(),
        P("slot", "blk", None),
        P("slot", "blk", None),
        P("slot", "blk", None),
        P("slot"),
    )
    return jax.shard_map(
        shards, mesh=mesh, in_specs=placed, out_specs=P("slot", "blk", None), check_vma=False
    )
```

```python
import jax
import jax.numpy as jnp
from jax import lax
from jax.experimental import pallas as pl
from jax.experimental.pallas import tpu as pltpu
from jax.sharding import PartitionSpec as P

COLS = 640
TOK = 640
BETA = 0.75
NZ = 16
NS = 16
ROWS = 112
KP = 128
PIECES = 7
MESH = pl.DeviceIdType.MESH
HOPS = NZ // 2
PARTS = (256, 384)
FIRST = (0, 256)
STREAMS = ((128, 128), (128, 128, 128))
LONG_UP = (0, 1, 2, 7)
A_STEPS = (
    ((0, 1),),
    ((0, 2),),
    ((0, 3),),
    ((0, 4),),
    ((0, 5),),
    ((0, 6),),
    ((0, 7), (1, 1)),
    ((0, 8), (1, 2)),
    ((1, 3),),
    ((1, 4),),
    ((1, 5),),
    ((1, 6),),
    ((1, 7),),
    ((1, 8),),
    (),
    (),
)
PRODUCTS = (
    (),
    ((0, 0, 0), (0, 0, 1), (0, 0, 2)),
    ((0, 0, 3),),
    ((0, 0, 4),),
    ((0, 0, 5),),
    (),
    (),
    (),
    ((0, 0, 6), (0, 0, 7), (0, 0, 8), (0, 1, 0)),
    ((2, 0, 0), (2, 0, 1), (2, 0, 2), (1, 0, 0), (1, 0, 1)),
    ((2, 0, 3), (1, 0, 2), (1, 0, 3), (1, 0, 4), (1, 0, 5), (1, 0, 6), (1, 0, 7), (1, 0, 8), (1, 1, 0)),
    ((2, 0, 4), (0, 1, 1), (1, 1, 1), (0, 1, 2), (1, 1, 2), (0, 1, 3), (1, 1, 3)),
    ((2, 0, 5), (0, 1, 4), (1, 1, 4), (0, 1, 5), (1, 1, 5), (0, 1, 6), (1, 1, 6)),
    ((2, 0, 6), (0, 1, 7), (1, 1, 7), (0, 1, 8), (1, 1, 8)),
    ((2, 0, 7),),
    (),
)
WHOLE = (11, 14)


def wait_for(ref, sem):
    pltpu.make_async_copy(ref, ref, sem).wait()


def kernel(
    owner_home, damping, factor, inverse, acts, out,
    owner, f_in, p_in, f_out, p_out, f_work, p_work, a_ring, a_w, p_a, p_a_sibling,
    w_ring, x_ring, total, sibling_part, fresh, gathered, picked,
    damp_out, damp_in, load_sem,
    swap_send, swap_recv, ring_send, ring_recv, pair_send, pair_recv,
    give_send, give_recv, pick_send, pick_recv, hello,
):
    slot = lax.axis_index("slot")
    blk = lax.axis_index("blk")
    chip = slot // 2
    core = slot % 2
    z = blk // 2
    side = blk % 2
    same = core == side

    def at(core_at, side_at, z_at):
        return (chip * 2 + core_at, z_at * 2 + side_at)

    sibling = at(1 - core, side, z)
    up = at(core, side, (z + 1) % NZ)
    down = at(core, side, (z + NZ - 1) % NZ)

    barrier = pltpu.get_barrier_semaphore()
    def other_chip(c, side_at):
        return (c * 2 + core, z * 2 + side_at)

    along_x = chip // 4 * 4
    far_partners = [
        other_chip((chip + 4) % 8, 1 - side),
        other_chip(along_x + chip % 4 // 2 * 2 + 1 - chip % 2, side),
        other_chip(along_x + 3 - chip % 4, side),
    ]
    partners = [up, down, sibling, at(core, 1 - side, z), at(1 - core, 1 - side, z)]
    swap_up = at(side, core, (z + 1) % NZ)
    swap_down = at(side, core, (z + NZ - 1) % NZ)

    @pl.when(jnp.logical_not(same))
    def _():
        for target in (swap_up, swap_down):
            pl.semaphore_signal(barrier, inc=1, device_id=target, device_id_type=MESH)

    for target in partners + far_partners:
        pl.semaphore_signal(barrier, inc=1, device_id=target, device_id_type=MESH)

    f_load = pltpu.make_async_copy(factor.at[0], f_in, load_sem.at[0])
    p_load = pltpu.make_async_copy(inverse.at[0], p_in, load_sem.at[1])
    f_load.start()
    p_load.start()
    owner_load = pltpu.make_async_copy(owner_home, owner, load_sem.at[2])
    owner_load.start()

    def greet(i):
        pl.semaphore_signal(
            hello.at[i], inc=1, device_id=far_partners[i], device_id_type=MESH
        )

    def greeted(i):
        pl.semaphore_wait(hello.at[i], 1)

    pending = []

    def keep(src, dst, recv, own):
        @pl.when(own)
        def _():
            pltpu.make_async_copy(src, dst, recv).start()

    def deliver(src, dst, send, recv, target, own, kept=False):
        pending.append(lambda: sent(src, send, own))

        if not kept:
            keep(src, dst, recv, own)

        @pl.when(jnp.logical_not(own))
        def _():
            pltpu.make_async_remote_copy(
                src_ref=src, dst_ref=dst, send_sem=send, recv_sem=recv,
                device_id=target, device_id_type=MESH,
            ).start()

    def sent(src, send, own):
        @pl.when(jnp.logical_not(own))
        def _():
            wait_for(src, send)

    w_pieces, first = [], 0
    for p in range(2):
        for q, width in enumerate(STREAMS[p]):
            w_pieces.append((p, q, first, width))
            first += width
    w_home = [inverse.at[0, :, pl.ds(first, width)] for p, q, first, width in w_pieces]
    a_home = [acts.at[0, :, pl.ds(FIRST[p], PARTS[p])] for p in range(2)]
    own_rows = pl.ds(pl.multiple_of(side * ROWS, 16), ROWS)

    for i, (p, q, _, _) in enumerate(w_pieces):
        keep(w_home[i], w_ring[p][q].at[z, pl.ds(0, ROWS)], swap_recv.at[i], same)
    for p in range(2):
        keep(a_home[p], a_ring[p].at[z, pl.ds(0, ROWS)], swap_recv.at[5 + p], same)

    pad = jnp.zeros((KP - ROWS, COLS), jnp.bfloat16)

    def clear(i, carry):
        for p in range(2):
            a_ring[p][i, ROWS:KP, :] = pad[:, : PARTS[p]]
            for q, width in enumerate(STREAMS[p]):
                w_ring[p][q][i, ROWS:KP, :] = pad[:, :width]
                x_ring[p][q][i, ROWS:KP, :] = pad[:, :width]
        return carry

    lax.fori_loop(0, NZ, clear, 0)
    def relayout(src, dst):
        for j in range(2 * NZ):
            start = ROWS * j
            base = start // 128 * 128
            off = start - base
            if off == 0:
                piece = src[:, base : base + 128].astype(jnp.bfloat16)
            elif off + ROWS <= 128:
                piece = pltpu.roll(
                    src[:, base : base + 128].astype(jnp.float32), 128 - off, 1
                ).astype(jnp.bfloat16)
            else:
                piece = pltpu.roll(
                    src[:, base : base + 256].astype(jnp.float32), 256 - off, 1
                )[:, :128].astype(jnp.bfloat16)
            dst[j % 2, j // 2] = piece

    @pl.when(same)
    def _():
        pl.semaphore_wait(barrier, len(partners) + len(far_partners))

    @pl.when(jnp.logical_not(same))
    def _():
        pl.semaphore_wait(barrier, len(partners) + len(far_partners) + 2)

    greet(0)

    def swap_w(i):
        p, q = w_pieces[i][:2]
        deliver(
            w_home[i], w_ring[p][q].at[z, pl.ds(0, ROWS)], swap_send.at[i],
            swap_recv.at[i], at(side, core, z), same, True,
        )

    def swap_a(p):
        deliver(
            a_home[p], a_ring[p].at[z, pl.ds(0, ROWS)], swap_send.at[5 + p],
            swap_recv.at[5 + p], at(side, core, z), same, True,
        )

    rings = [a_ring[0], a_ring[1]] + [w_ring[p][q] for p, q, _, _ in w_pieces]
    w_streams = range(2, len(rings))
    streams_of = []
    for p in range(2):
        streams_of.append(range(len(rings), len(rings) + len(STREAMS[p])))
        rings += [x_ring[p][q] for q in range(len(STREAMS[p]))]

    def ring_ref(stream, place):
        return rings[stream].at[place, pl.ds(0, ROWS)]

    def far(stream):
        return (HOPS, HOPS - 1) if stream in LONG_UP else (HOPS - 1, HOPS)

    def place_of(way, hop):
        return (z - hop + NZ) % NZ if way == 0 else (z + hop) % NZ

    def first_hop(stream):
        home = w_home[stream - 2] if stream >= 2 else a_home[stream]
        for way in range(2):
            pltpu.make_async_remote_copy(
                src_ref=home, dst_ref=ring_ref(stream, z),
                send_sem=ring_send.at[stream, way, 0], recv_sem=ring_recv.at[stream, z],
                device_id=swap_up if way == 0 else swap_down, device_id_type=MESH,
            ).start()
            pending.append(lambda r=home, m=ring_send.at[stream, way, 0]: wait_for(r, m))

    for stream in w_streams:
        first_hop(stream)
    first_hop(0)
    for i in range(len(w_pieces)):
        swap_w(i)
    swap_a(0)

    damp_out[...] = jnp.full((8, 128), damping[0], jnp.float32)

    @pl.when(same)
    def _():
        damp_in[...] = damp_out[...]
        pltpu.make_async_remote_copy(
            src_ref=damp_out, dst_ref=damp_in, send_sem=swap_send.at[11],
            recv_sem=swap_recv.at[11], device_id=sibling, device_id_type=MESH,
        ).start()

    def send_panel(src, dst, first):
        for q in range(2):
            deliver(
                src.at[q], dst.at[:, own_rows], swap_send.at[first + q],
                swap_recv.at[first + side],
                at(q, core, z), jnp.logical_and(same, core == q),
            )

    def step(stream, hop):
        for way in range(2):
            if hop <= far(stream)[way]:
                place = place_of(way, hop)
                ref = ring_ref(stream, place)
                if hop > 0:
                    wait_for(ref, ring_recv.at[stream, place])
                if hop < far(stream)[way]:
                    pltpu.make_async_remote_copy(
                        src_ref=ref, dst_ref=ref, send_sem=ring_send.at[stream, way, hop],
                        recv_sem=ring_recv.at[stream, place],
                        device_id=up if way == 0 else down, device_id_type=MESH,
                    ).start()
                    pending.append(
                        lambda r=ref, m=ring_send.at[stream, way, hop]: wait_for(r, m)
                    )

    def rows_of(ring, places):
        return jnp.concatenate([ring[place] for place in places], axis=0)

    def lanes_of(panel, places):
        return jnp.concatenate([panel[place] for place in places], axis=1)

    def outer_product(p, places):
        window = jnp.concatenate(
            [rows_of(w_ring[i][q], places) for i, q, _, _ in w_pieces], axis=1
        )
        a_w[p][...] += lax.dot_general(
            rows_of(a_ring[p], places), window, (((0,), (0,)), ((), ())),
            preferred_element_type=jnp.float32,
        )

    def acts_product(p, places):
        p_a[p][...] += jnp.dot(
            lanes_of(p_work, places), rows_of(a_ring[p], places),
            preferred_element_type=jnp.float32,
        )

    def panel_product(panel, ring, p, places):
        first = 0
        blocks = lanes_of(panel, places)
        for q, width in enumerate(STREAMS[p]):
            total[p][:, first : first + width] += jnp.dot(
                blocks, rows_of(ring[p][q], places), preferred_element_type=jnp.float32
            )
            first += width

    def first_product(p, places):
        panel_product(f_work, w_ring, p, places)

    def second_product(p, places):
        panel_product(p_work, x_ring, p, places)

    def both(product, p, hop):
        if hop == 0 or hop == HOPS:
            product(p, [(z + hop) % NZ])
        else:
            product(p, [(z + NZ - hop) % NZ, (z + hop) % NZ])

    def work(g):
        for kind, p, hop in PRODUCTS[g - 1]:
            if kind == 0:
                both(outer_product, p, hop)
            elif kind == 1:
                both(acts_product, p, hop)
            else:
                for q in range(2):
                    both(second_product, q, hop)

    mine = pl.ds(pl.multiple_of(core * ROWS, 16), ROWS)
    other = pl.ds(pl.multiple_of((1 - core) * ROWS, 16), ROWS)

    def pair_copy(p, phase):
        return pltpu.make_async_remote_copy(
            src_ref=total[p].at[other], dst_ref=sibling_part[p].at[phase],
            send_sem=pair_send.at[p, phase], recv_sem=pair_recv.at[p, phase],
            device_id=sibling, device_id_type=MESH,
        )

    f_load.wait()
    relayout(f_in, f_out)
    send_panel(f_out, f_work, 7)
    p_load.wait()
    owner_load.wait()
    relayout(p_in, p_out)
    for p in range(2):
        total[p][...] = jnp.zeros_like(total[p])

    for p in range(2):
        p_a[p][...] = jnp.zeros_like(p_a[p])
        a_w[p][...] = jnp.zeros_like(a_w[p])

    for hop in range(1, HOPS + 1):
        for stream in w_streams:
            step(stream, hop)
        if hop == HOPS:
            for p in range(2):
                both(first_product, p, hop)
                pair_copy(p, 0).start()
        else:
            for p, h in A_STEPS[hop - 1]:
                step(p, h)
        if hop in (2, 4, 6):
            greeted(hop // 2 - 1)
            if hop < 6:
                greet(hop // 2)
        if hop == 4:
            swap_a(1)
            first_hop(1)
        if hop == 2:
            for i, (p, q, _, _) in enumerate(w_pieces):
                wait_for(w_ring[p][q].at[z, pl.ds(0, ROWS)], swap_recv.at[i])
            wait_for(a_ring[0].at[z, pl.ds(0, ROWS)], swap_recv.at[5])
        if hop == 7:
            wait_for(rings[1].at[z, pl.ds(0, ROWS)], swap_recv.at[6])
        if hop == 3:
            send_panel(p_out, p_work, 9)
        if hop == 5:
            for b in range(2):
                wait_for(f_work.at[:, pl.ds(b * ROWS, ROWS)], swap_recv.at[7 + b])
        if 5 <= hop < HOPS:
            for h in range(3 * hop - 15, min(3 * hop - 12, HOPS)):
                for p in range(2):
                    both(first_product, p, h)
        work(hop)

    @pl.when(jnp.logical_not(same))
    def _():
        wait_for(damp_in, swap_recv.at[11])

    def own_window(p):
        return jnp.concatenate(
            [ring[z, 0:ROWS, :] for ring in w_ring[p]], axis=1
        ).astype(jnp.float32)

    def apply(p):
        pair_copy(p, 0).wait()
        window = own_window(p)
        applied = BETA * (total[p][mine, :] + sibling_part[p][0])
        applied = applied + damp_in[0:1, 0:1] * window
        applied = applied.astype(jnp.bfloat16)
        first = 0
        for q, width in enumerate(STREAMS[p]):
            x_ring[p][q][z, 0:ROWS, :] = applied[:, first : first + width]
            step(streams_of[p][q], 0)
            first += width
        total[p][...] = jnp.zeros_like(total[p])

    apply(0)
    apply(1)
    for p, h in A_STEPS[HOPS - 1]:
        step(p, h)

    def acts_copy(p):
        return pltpu.make_async_remote_copy(
            src_ref=p_a[p], dst_ref=p_a_sibling[p], send_sem=pair_send.at[p, 2],
            recv_sem=pair_recv.at[p, 2], device_id=sibling, device_id_type=MESH,
        )

    def join(p):
        acts_copy(p).wait()
        rows = ((1.0 - BETA) / TOK) * (p_a[p][...] + p_a_sibling[p][...])
        share = jnp.dot(
            rows.astype(jnp.bfloat16), a_w[p][...].astype(jnp.bfloat16),
            preferred_element_type=jnp.float32,
        )
        for q in range(2):
            total[q][...] += share[:, FIRST[q] : FIRST[q] + PARTS[q]]

    early, pending[:] = list(pending), []
    for hop in range(1, HOPS + 1):
        if hop == HOPS:
            join(0)
            join(1)
        for p in range(2):
            for stream in streams_of[p]:
                step(stream, hop)
            if hop == HOPS:
                both(second_product, p, hop)
                pair_copy(p, 1).start()
        for p, h in A_STEPS[HOPS + hop - 1]:
            step(p, h)
        if hop == 2:
            for b in range(2):
                wait_for(p_work.at[:, pl.ds(b * ROWS, ROWS)], swap_recv.at[9 + b])
        work(HOPS + hop)
        for p in range(2):
            if WHOLE[p] == HOPS + hop:
                acts_copy(p).start()
        for left in early[(hop - 1) * len(early) // 6 : hop * len(early) // 6]:
            left()

    layer = chip * 2 + side
    for p in range(2):
        pair_copy(p, 1).wait()
        window = own_window(p)
        fresh[p][...] = (
            2.0 * window - (total[p][mine, :] + sibling_part[p][1])
        ).astype(jnp.bfloat16)
        for r in range(PIECES):
            target = 2 * r + p
            deliver(
                fresh[p].at[pl.ds(r * 16, 16)], gathered[p].at[layer],
                give_send.at[p, r], give_recv.at[p, layer], (target, z * 2 + core),
                jnp.logical_and(slot == target, side == core),
            )

    for left in pending[:-2 * PIECES]:
        left()
    pending[:] = pending[-2 * PIECES :]

    def middle(p):
        return jnp.logical_and(chip < PIECES, core == p)

    piece_rows = pl.ds(pl.multiple_of((chip % PIECES) * 16, 16), 16)
    for p in range(2):
        @pl.when(middle(p))
        def _():
            for layer_at in range(NS):
                wait_for(gathered[p].at[layer_at], give_recv.at[p, layer_at])
            for l in range(NS):
                picked[p][l * 16 : (l + 1) * 16, :] = gathered[p][owner[l]]
                deliver(
                    picked[p].at[pl.ds(l * 16, 16)],
                    out.at[0, piece_rows, pl.ds(FIRST[p], PARTS[p])],
                    pick_send.at[p, l], pick_recv.at[p, chip], (l, blk), slot == l,
                )
                pending.pop()

    for left in pending:
        left()

    @pl.when(same)
    def _():
        wait_for(damp_out, swap_send.at[11])

    for p in range(2):
        @pl.when(middle(p))
        def _():
            for l in range(NS):
                sent(picked[p].at[pl.ds(l * 16, 16)], pick_send.at[p, l], slot == l)

    for p in range(2):
        for r in range(PIECES):
            wait_for(
                out.at[0, pl.ds(r * 16, 16), pl.ds(FIRST[p], PARTS[p])], pick_recv.at[p, r]
            )


def shards(owner, factor, inverse_old, acts_t, damping):
    bf16, f32 = jnp.bfloat16, jnp.float32
    dma, vmem = pltpu.SemaphoreType.DMA, pltpu.VMEM
    n_streams = 2 + 2 * sum(len(widths) for widths in STREAMS)
    width = factor.shape[2]
    smem = pl.BlockSpec(memory_space=pltpu.SMEM)
    anywhere = pl.BlockSpec(memory_space=pltpu.HBM)
    return pl.pallas_call(
        kernel,
        out_shape=jax.ShapeDtypeStruct((1, ROWS, COLS), bf16),
        in_specs=[anywhere, smem, anywhere, anywhere, anywhere],
        out_specs=anywhere,
        scratch_shapes=[
            pltpu.SMEM((NS,), jnp.int32),
            vmem((ROWS, width), f32),
            vmem((ROWS, width), bf16),
            vmem((2, NZ, ROWS, KP), bf16),
            vmem((2, NZ, ROWS, KP), bf16),
            vmem((NZ, 2 * ROWS, KP), bf16),
            vmem((NZ, 2 * ROWS, KP), bf16),
            [vmem((NZ, KP, n), bf16) for n in PARTS],
            [vmem((n, COLS), f32) for n in PARTS],
            [vmem((2 * ROWS, n), f32) for n in PARTS],
            [vmem((2 * ROWS, n), f32) for n in PARTS],
            [[vmem((NZ, KP, n), bf16) for n in widths] for widths in STREAMS],
            [[vmem((NZ, KP, n), bf16) for n in widths] for widths in STREAMS],
            [vmem((2 * ROWS, n), f32) for n in PARTS],
            [vmem((2, ROWS, n), f32) for n in PARTS],
            [vmem((ROWS, n), bf16) for n in PARTS],
            [vmem((NS, 16, n), bf16) for n in PARTS],
            [vmem((NS * 16, n), bf16) for n in PARTS],
            vmem((8, 128), f32),
            vmem((8, 128), f32),
            dma((3,)),
            dma((12,)),
            dma((12,)),
            dma((n_streams, 2, HOPS)),
            dma((n_streams, NZ)),
            dma((2, 3)),
            dma((2, 3)),
            dma((2, PIECES)),
            dma((2, NS)),
            dma((2, NS)),
            dma((2, PIECES)),
            pltpu.SemaphoreType.REGULAR((3,)),
        ],
        compiler_params=pltpu.CompilerParams(
            collective_id=0, has_side_effects=True, vmem_limit_bytes=60 * 1024 * 1024
        ),
        cost_estimate=pl.CostEstimate(
            flops=2 * 3 * ROWS * width * COLS, bytes_accessed=3 * 1024 * 1024, transcendentals=0
        ),
    )(owner, damping, factor, inverse_old, acts_t)


def solution(mesh):
    placed = (
        P(),
        P("slot", "blk", None),
        P("slot", "blk", None),
        P("slot", "blk", None),
        P("slot"),
    )
    return jax.shard_map(
        shards, mesh=mesh, in_specs=placed, out_specs=P("slot", "blk", None), check_vma=False
    )
```

```python
import jax
import jax.numpy as jnp
from jax import lax
from jax.experimental import pallas as pl
from jax.experimental.pallas import tpu as pltpu
from jax.sharding import PartitionSpec as P

COLS = 640
TOK = 640
BETA = 0.75
NZ = 16
NS = 16
ROWS = 112
KP = 128
PIECES = 7
MESH = pl.DeviceIdType.MESH
HOPS = NZ // 2
PARTS = (256, 384)
FIRST = (0, 256)
STREAMS = ((128, 128), (128, 128, 128))
LONG_UP = (0, 1, 2, 4, 7, 9)
A_STEPS = (
    ((0, 1),),
    ((0, 2),),
    ((0, 3),),
    ((0, 4),),
    ((0, 5),),
    ((0, 6),),
    ((0, 7), (1, 1)),
    ((0, 8), (1, 2)),
    ((1, 3),),
    ((1, 4),),
    ((1, 5),),
    ((1, 6),),
    ((1, 7),),
    ((1, 8),),
    (),
    (),
)
PRODUCTS = (
    (),
    ((0, 0, 0), (0, 0, 1), (0, 0, 2)),
    ((0, 0, 3),),
    ((0, 0, 4),),
    ((0, 0, 5),),
    (),
    (),
    (),
    ((0, 0, 6), (0, 0, 7), (0, 0, 8), (0, 1, 0)),
    ((2, 0, 0), (2, 0, 1), (2, 0, 2), (1, 0, 0), (1, 0, 1)),
    ((2, 0, 3), (1, 0, 2), (1, 0, 3), (1, 0, 4), (1, 0, 5), (1, 0, 6), (1, 0, 7), (1, 0, 8), (1, 1, 0)),
    ((2, 0, 4), (0, 1, 1), (1, 1, 1), (0, 1, 2), (1, 1, 2), (0, 1, 3), (1, 1, 3)),
    ((2, 0, 5), (0, 1, 4), (1, 1, 4), (0, 1, 5), (1, 1, 5), (0, 1, 6), (1, 1, 6)),
    ((2, 0, 6), (0, 1, 7), (1, 1, 7), (0, 1, 8), (1, 1, 8)),
    ((2, 0, 7),),
    (),
)
WHOLE = (11, 14)


def wait_for(ref, sem):
    pltpu.make_async_copy(ref, ref, sem).wait()


def kernel(
    owner_home, damping, factor, inverse, acts, out,
    owner, f_in, p_in, f_out, p_out, f_work, p_work, a_ring, a_w, p_a, p_a_sibling,
    w_ring, x_ring, total, sibling_part, fresh, gathered, picked,
    damp_out, damp_in, load_sem,
    swap_send, swap_recv, ring_send, ring_recv, pair_send, pair_recv,
    give_send, give_recv, pick_send, pick_recv, hello,
):
    slot = lax.axis_index("slot")
    blk = lax.axis_index("blk")
    chip = slot // 2
    core = slot % 2
    z = blk // 2
    side = blk % 2
    same = core == side

    def at(core_at, side_at, z_at):
        return (chip * 2 + core_at, z_at * 2 + side_at)

    sibling = at(1 - core, side, z)
    up = at(core, side, (z + 1) % NZ)
    down = at(core, side, (z + NZ - 1) % NZ)

    barrier = pltpu.get_barrier_semaphore()
    def other_chip(c, side_at):
        return (c * 2 + core, z * 2 + side_at)

    along_x = chip // 4 * 4
    far_partners = [
        other_chip((chip + 4) % 8, 1 - side),
        other_chip(along_x + chip % 4 // 2 * 2 + 1 - chip % 2, side),
        other_chip(along_x + 3 - chip % 4, side),
    ]
    partners = [up, down, sibling, at(core, 1 - side, z), at(1 - core, 1 - side, z)]
    swap_up = at(side, core, (z + 1) % NZ)
    swap_down = at(side, core, (z + NZ - 1) % NZ)

    @pl.when(jnp.logical_not(same))
    def _():
        for target in (swap_up, swap_down):
            pl.semaphore_signal(barrier, inc=1, device_id=target, device_id_type=MESH)

    for target in partners + far_partners:
        pl.semaphore_signal(barrier, inc=1, device_id=target, device_id_type=MESH)

    f_load = pltpu.make_async_copy(factor.at[0], f_in, load_sem.at[0])
    p_load = pltpu.make_async_copy(inverse.at[0], p_in, load_sem.at[1])
    f_load.start()
    p_load.start()
    owner_load = pltpu.make_async_copy(owner_home, owner, load_sem.at[2])
    owner_load.start()

    def greet(i):
        pl.semaphore_signal(
            hello.at[i], inc=1, device_id=far_partners[i], device_id_type=MESH
        )

    def greeted(i):
        pl.semaphore_wait(hello.at[i], 1)

    pending = []

    def keep(src, dst, recv, own):
        @pl.when(own)
        def _():
            pltpu.make_async_copy(src, dst, recv).start()

    def deliver(src, dst, send, recv, target, own, kept=False):
        pending.append(lambda: sent(src, send, own))

        if not kept:
            keep(src, dst, recv, own)

        @pl.when(jnp.logical_not(own))
        def _():
            pltpu.make_async_remote_copy(
                src_ref=src, dst_ref=dst, send_sem=send, recv_sem=recv,
                device_id=target, device_id_type=MESH,
            ).start()

    def sent(src, send, own):
        @pl.when(jnp.logical_not(own))
        def _():
            wait_for(src, send)

    w_pieces, first = [], 0
    for p in range(2):
        for q, width in enumerate(STREAMS[p]):
            w_pieces.append((p, q, first, width))
            first += width
    w_home = [inverse.at[0, :, pl.ds(first, width)] for p, q, first, width in w_pieces]
    a_home = [acts.at[0, :, pl.ds(FIRST[p], PARTS[p])] for p in range(2)]
    own_rows = pl.ds(pl.multiple_of(side * ROWS, 16), ROWS)

    for i, (p, q, _, _) in enumerate(w_pieces):
        keep(w_home[i], w_ring[p][q].at[z, pl.ds(0, ROWS)], swap_recv.at[i], same)
    for p in range(2):
        keep(a_home[p], a_ring[p].at[z, pl.ds(0, ROWS)], swap_recv.at[5 + p], same)

    pad = jnp.zeros((KP - ROWS, COLS), jnp.bfloat16)

    def clear(i, carry):
        for p in range(2):
            a_ring[p][i, ROWS:KP, :] = pad[:, : PARTS[p]]
            for q, width in enumerate(STREAMS[p]):
                w_ring[p][q][i, ROWS:KP, :] = pad[:, :width]
                x_ring[p][q][i, ROWS:KP, :] = pad[:, :width]
        return carry

    lax.fori_loop(0, NZ, clear, 0)
    def relayout(src, dst):
        for j in range(2 * NZ):
            start = ROWS * j
            base = start // 128 * 128
            off = start - base
            if off == 0:
                piece = src[:, base : base + 128].astype(jnp.bfloat16)
            elif off + ROWS <= 128:
                piece = pltpu.roll(
                    src[:, base : base + 128].astype(jnp.float32), 128 - off, 1
                ).astype(jnp.bfloat16)
            else:
                piece = pltpu.roll(
                    src[:, base : base + 256].astype(jnp.float32), 256 - off, 1
                )[:, :128].astype(jnp.bfloat16)
            dst[j % 2, j // 2] = piece

    @pl.when(same)
    def _():
        pl.semaphore_wait(barrier, len(partners) + len(far_partners))

    @pl.when(jnp.logical_not(same))
    def _():
        pl.semaphore_wait(barrier, len(partners) + len(far_partners) + 2)

    greet(0)

    def swap_w(i):
        p, q = w_pieces[i][:2]
        deliver(
            w_home[i], w_ring[p][q].at[z, pl.ds(0, ROWS)], swap_send.at[i],
            swap_recv.at[i], at(side, core, z), same, True,
        )

    def swap_a(p):
        deliver(
            a_home[p], a_ring[p].at[z, pl.ds(0, ROWS)], swap_send.at[5 + p],
            swap_recv.at[5 + p], at(side, core, z), same, True,
        )

    rings = [a_ring[0], a_ring[1]] + [w_ring[p][q] for p, q, _, _ in w_pieces]
    w_streams = range(2, len(rings))
    streams_of = []
    for p in range(2):
        streams_of.append(range(len(rings), len(rings) + len(STREAMS[p])))
        rings += [x_ring[p][q] for q in range(len(STREAMS[p]))]

    def ring_ref(stream, place):
        return rings[stream].at[place, pl.ds(0, ROWS)]

    def far(stream):
        return (HOPS, HOPS - 1) if stream in LONG_UP else (HOPS - 1, HOPS)

    def place_of(way, hop):
        return (z - hop + NZ) % NZ if way == 0 else (z + hop) % NZ

    def first_hop(stream):
        home = w_home[stream - 2] if stream >= 2 else a_home[stream]
        for way in range(2):
            pltpu.make_async_remote_copy(
                src_ref=home, dst_ref=ring_ref(stream, z),
                send_sem=ring_send.at[stream, way, 0], recv_sem=ring_recv.at[stream, z],
                device_id=swap_up if way == 0 else swap_down, device_id_type=MESH,
            ).start()
            pending.append(lambda r=home, m=ring_send.at[stream, way, 0]: wait_for(r, m))

    for stream in w_streams:
        first_hop(stream)
    first_hop(0)
    for i in range(len(w_pieces)):
        swap_w(i)
    swap_a(0)

    damp_out[...] = jnp.full((8, 128), damping[0], jnp.float32)

    @pl.when(same)
    def _():
        damp_in[...] = damp_out[...]
        pltpu.make_async_remote_copy(
            src_ref=damp_out, dst_ref=damp_in, send_sem=swap_send.at[11],
            recv_sem=swap_recv.at[11], device_id=sibling, device_id_type=MESH,
        ).start()

    def send_panel(src, dst, first):
        for q in range(2):
            deliver(
                src.at[q], dst.at[:, own_rows], swap_send.at[first + q],
                swap_recv.at[first + side],
                at(q, core, z), jnp.logical_and(same, core == q),
            )

    def step(stream, hop):
        for way in range(2):
            if hop <= far(stream)[way]:
                place = place_of(way, hop)
                ref = ring_ref(stream, place)
                if hop > 0:
                    wait_for(ref, ring_recv.at[stream, place])
                if hop < far(stream)[way]:
                    pltpu.make_async_remote_copy(
                        src_ref=ref, dst_ref=ref, send_sem=ring_send.at[stream, way, hop],
                        recv_sem=ring_recv.at[stream, place],
                        device_id=up if way == 0 else down, device_id_type=MESH,
                    ).start()
                    pending.append(
                        lambda r=ref, m=ring_send.at[stream, way, hop]: wait_for(r, m)
                    )

    def rows_of(ring, places):
        return jnp.concatenate([ring[place] for place in places], axis=0)

    def lanes_of(panel, places):
        return jnp.concatenate([panel[place] for place in places], axis=1)

    def outer_product(p, places):
        window = jnp.concatenate(
            [rows_of(w_ring[i][q], places) for i, q, _, _ in w_pieces], axis=1
        )
        a_w[p][...] += lax.dot_general(
            rows_of(a_ring[p], places), window, (((0,), (0,)), ((), ())),
            preferred_element_type=jnp.float32,
        )

    def acts_product(p, places):
        p_a[p][...] += jnp.dot(
            lanes_of(p_work, places), rows_of(a_ring[p], places),
            preferred_element_type=jnp.float32,
        )

    def panel_product(panel, ring, p, places):
        first = 0
        blocks = lanes_of(panel, places)
        for q, width in enumerate(STREAMS[p]):
            total[p][:, first : first + width] += jnp.dot(
                blocks, rows_of(ring[p][q], places), preferred_element_type=jnp.float32
            )
            first += width

    def first_product(p, places):
        panel_product(f_work, w_ring, p, places)

    def second_product(p, places):
        panel_product(p_work, x_ring, p, places)

    def both(product, p, hop):
        if hop == 0 or hop == HOPS:
            product(p, [(z + hop) % NZ])
        else:
            product(p, [(z + NZ - hop) % NZ, (z + hop) % NZ])

    def work(g):
        for kind, p, hop in PRODUCTS[g - 1]:
            if kind == 0:
                both(outer_product, p, hop)
            elif kind == 1:
                both(acts_product, p, hop)
            else:
                for q in range(2):
                    both(second_product, q, hop)

    mine = pl.ds(pl.multiple_of(core * ROWS, 16), ROWS)
    other = pl.ds(pl.multiple_of((1 - core) * ROWS, 16), ROWS)

    def pair_copy(p, phase):
        return pltpu.make_async_remote_copy(
            src_ref=total[p].at[other], dst_ref=sibling_part[p].at[phase],
            send_sem=pair_send.at[p, phase], recv_sem=pair_recv.at[p, phase],
            device_id=sibling, device_id_type=MESH,
        )

    f_load.wait()
    relayout(f_in, f_out)
    send_panel(f_out, f_work, 7)
    p_load.wait()
    owner_load.wait()
    relayout(p_in, p_out)
    for p in range(2):
        total[p][...] = jnp.zeros_like(total[p])

    for p in range(2):
        p_a[p][...] = jnp.zeros_like(p_a[p])
        a_w[p][...] = jnp.zeros_like(a_w[p])

    for hop in range(1, HOPS + 1):
        for stream in w_streams:
            step(stream, hop)
        if hop == HOPS:
            for p in range(2):
                both(first_product, p, hop)
                pair_copy(p, 0).start()
        else:
            for p, h in A_STEPS[hop - 1]:
                step(p, h)
        if hop in (2, 4, 6):
            greeted(hop // 2 - 1)
            if hop < 6:
                greet(hop // 2)
        if hop == 4:
            swap_a(1)
            first_hop(1)
        if hop == 2:
            for i, (p, q, _, _) in enumerate(w_pieces):
                wait_for(w_ring[p][q].at[z, pl.ds(0, ROWS)], swap_recv.at[i])
            wait_for(a_ring[0].at[z, pl.ds(0, ROWS)], swap_recv.at[5])
        if hop == 7:
            wait_for(rings[1].at[z, pl.ds(0, ROWS)], swap_recv.at[6])
        if hop == 3:
            send_panel(p_out, p_work, 9)
        if hop == 5:
            for b in range(2):
                wait_for(f_work.at[:, pl.ds(b * ROWS, ROWS)], swap_recv.at[7 + b])
        if 5 <= hop < HOPS:
            for h in range(3 * hop - 15, min(3 * hop - 12, HOPS)):
                for p in range(2):
                    both(first_product, p, h)
        work(hop)

    @pl.when(jnp.logical_not(same))
    def _():
        wait_for(damp_in, swap_recv.at[11])

    def own_window(p):
        return jnp.concatenate(
            [ring[z, 0:ROWS, :] for ring in w_ring[p]], axis=1
        ).astype(jnp.float32)

    def apply(p):
        pair_copy(p, 0).wait()
        window = own_window(p)
        applied = BETA * (total[p][mine, :] + sibling_part[p][0])
        applied = applied + damp_in[0:1, 0:1] * window
        applied = applied.astype(jnp.bfloat16)
        first = 0
        for q, width in enumerate(STREAMS[p]):
            x_ring[p][q][z, 0:ROWS, :] = applied[:, first : first + width]
            step(streams_of[p][q], 0)
            first += width
        total[p][...] = jnp.zeros_like(total[p])

    apply(0)
    apply(1)
    for p, h in A_STEPS[HOPS - 1]:
        step(p, h)

    def acts_copy(p):
        return pltpu.make_async_remote_copy(
            src_ref=p_a[p], dst_ref=p_a_sibling[p], send_sem=pair_send.at[p, 2],
            recv_sem=pair_recv.at[p, 2], device_id=sibling, device_id_type=MESH,
        )

    def join(p):
        acts_copy(p).wait()
        rows = ((1.0 - BETA) / TOK) * (p_a[p][...] + p_a_sibling[p][...])
        share = jnp.dot(
            rows.astype(jnp.bfloat16), a_w[p][...].astype(jnp.bfloat16),
            preferred_element_type=jnp.float32,
        )
        for q in range(2):
            total[q][...] += share[:, FIRST[q] : FIRST[q] + PARTS[q]]

    early, pending[:] = list(pending), []
    for hop in range(1, HOPS + 1):
        if hop == HOPS:
            join(0)
            join(1)
        for p in range(2):
            for stream in streams_of[p]:
                step(stream, hop)
            if hop == HOPS:
                both(second_product, p, hop)
                pair_copy(p, 1).start()
        for p, h in A_STEPS[HOPS + hop - 1]:
            step(p, h)
        if hop == 2:
            for b in range(2):
                wait_for(p_work.at[:, pl.ds(b * ROWS, ROWS)], swap_recv.at[9 + b])
        work(HOPS + hop)
        for p in range(2):
            if WHOLE[p] == HOPS + hop:
                acts_copy(p).start()
        for left in early[(hop - 1) * len(early) // 6 : hop * len(early) // 6]:
            left()

    layer = chip * 2 + side
    for p in range(2):
        pair_copy(p, 1).wait()
        window = own_window(p)
        fresh[p][...] = (
            2.0 * window - (total[p][mine, :] + sibling_part[p][1])
        ).astype(jnp.bfloat16)
        for r in range(PIECES):
            target = 2 * r + p
            deliver(
                fresh[p].at[pl.ds(r * 16, 16)], gathered[p].at[layer],
                give_send.at[p, r], give_recv.at[p, layer], (target, z * 2 + core),
                jnp.logical_and(slot == target, side == core),
            )

    for left in pending[:-2 * PIECES]:
        left()
    pending[:] = pending[-2 * PIECES :]

    def middle(p):
        return jnp.logical_and(chip < PIECES, core == p)

    piece_rows = pl.ds(pl.multiple_of((chip % PIECES) * 16, 16), 16)
    for p in range(2):
        @pl.when(middle(p))
        def _():
            for layer_at in range(NS):
                wait_for(gathered[p].at[layer_at], give_recv.at[p, layer_at])
            for l in range(NS):
                picked[p][l * 16 : (l + 1) * 16, :] = gathered[p][owner[l]]
                deliver(
                    picked[p].at[pl.ds(l * 16, 16)],
                    out.at[0, piece_rows, pl.ds(FIRST[p], PARTS[p])],
                    pick_send.at[p, l], pick_recv.at[p, chip], (l, blk), slot == l,
                )
                pending.pop()

    for left in pending:
        left()

    @pl.when(same)
    def _():
        wait_for(damp_out, swap_send.at[11])

    for p in range(2):
        @pl.when(middle(p))
        def _():
            for l in range(NS):
                sent(picked[p].at[pl.ds(l * 16, 16)], pick_send.at[p, l], slot == l)

    for p in range(2):
        for r in range(PIECES):
            wait_for(
                out.at[0, pl.ds(r * 16, 16), pl.ds(FIRST[p], PARTS[p])], pick_recv.at[p, r]
            )


def shards(owner, factor, inverse_old, acts_t, damping):
    bf16, f32 = jnp.bfloat16, jnp.float32
    dma, vmem = pltpu.SemaphoreType.DMA, pltpu.VMEM
    n_streams = 2 + 2 * sum(len(widths) for widths in STREAMS)
    width = factor.shape[2]
    smem = pl.BlockSpec(memory_space=pltpu.SMEM)
    anywhere = pl.BlockSpec(memory_space=pltpu.HBM)
    return pl.pallas_call(
        kernel,
        out_shape=jax.ShapeDtypeStruct((1, ROWS, COLS), bf16),
        in_specs=[anywhere, smem, anywhere, anywhere, anywhere],
        out_specs=anywhere,
        scratch_shapes=[
            pltpu.SMEM((NS,), jnp.int32),
            vmem((ROWS, width), f32),
            vmem((ROWS, width), bf16),
            vmem((2, NZ, ROWS, KP), bf16),
            vmem((2, NZ, ROWS, KP), bf16),
            vmem((NZ, 2 * ROWS, KP), bf16),
            vmem((NZ, 2 * ROWS, KP), bf16),
            [vmem((NZ, KP, n), bf16) for n in PARTS],
            [vmem((n, COLS), f32) for n in PARTS],
            [vmem((2 * ROWS, n), f32) for n in PARTS],
            [vmem((2 * ROWS, n), f32) for n in PARTS],
            [[vmem((NZ, KP, n), bf16) for n in widths] for widths in STREAMS],
            [[vmem((NZ, KP, n), bf16) for n in widths] for widths in STREAMS],
            [vmem((2 * ROWS, n), f32) for n in PARTS],
            [vmem((2, ROWS, n), f32) for n in PARTS],
            [vmem((ROWS, n), bf16) for n in PARTS],
            [vmem((NS, 16, n), bf16) for n in PARTS],
            [vmem((NS * 16, n), bf16) for n in PARTS],
            vmem((8, 128), f32),
            vmem((8, 128), f32),
            dma((3,)),
            dma((12,)),
            dma((12,)),
            dma((n_streams, 2, HOPS)),
            dma((n_streams, NZ)),
            dma((2, 3)),
            dma((2, 3)),
            dma((2, PIECES)),
            dma((2, NS)),
            dma((2, NS)),
            dma((2, PIECES)),
            pltpu.SemaphoreType.REGULAR((3,)),
        ],
        compiler_params=pltpu.CompilerParams(
            collective_id=0, has_side_effects=True, vmem_limit_bytes=60 * 1024 * 1024
        ),
        cost_estimate=pl.CostEstimate(
            flops=2 * 3 * ROWS * width * COLS, bytes_accessed=3 * 1024 * 1024, transcendentals=0
        ),
    )(owner, damping, factor, inverse_old, acts_t)


def solution(mesh):
    placed = (
        P(),
        P("slot", "blk", None),
        P("slot", "blk", None),
        P("slot", "blk", None),
        P("slot"),
    )
    return jax.shard_map(
        shards, mesh=mesh, in_specs=placed, out_specs=P("slot", "blk", None), check_vma=False
    )
```
